256 devices in a mesh: freq: 8 (over y, z_lo), brick: 32 (over x, z_hi, core).
Axes of the slice: x: 4, y: 4, z: 8 (z_hi: 4, z_lo: 2; z = z_hi * 2 + z_lo), core: 2. Of those that a mesh axis runs over, the one named last changes fastest.
Arguments:
- forward: bfloat16 [8, 4, 6, 64, 1024], P('freq', None, None, 'brick'), may hold values from -6 to 6
- adjoint: bfloat16 [8, 160, 6, 64, 1024], P('freq', None, None, 'brick'), may hold values from -8 to 8
- probes: bfloat16 [64, 1024, 128], P('brick'), may hold values from -0.0234375 to 0.0234375
- datum: int32 [8, 256], P('freq'), may hold values from 0 to 319, as said below
Outputs:
- cell_basis: float32 [128, 64, 1024], P('freq', 'brick')
The draws below stay inside these ranges and needn't reach their ends.
Inputs may be any that keep to these rules, and one draw needn't show every extreme that they name: `datum`: the 256 codes of one group are distinct.
All inputs are finite; a program needn't handle non-finite values.
Results may differ from the reference program's by a relative error of at most 0.013.
Values may be sent and summed in bfloat16 or wider, within the bound.
No kernel may reach another device: no remote copies, remote signals or barrier semaphores. Data moves between devices by JAX's collectives and lax.ppermute only.
A program may use at most 128 MiB of HBM per device.

```python
import jax
import jax.numpy as jnp
from jax import lax

PROBES = 128
PANEL = 256
FQ = 2
SITES = 40
NX = 64
ITERS = 4
GROUPS = 8
NF = 4
NXY = 1024
NZ = 64


def draw_adjoint(key, part):
    key = jax.random.fold_in(key, 3)
    keys = jax.random.split(key, 3)
    shape = (GROUPS, FQ, SITES, 2, 6, NZ, NXY)
    common_shape = (GROUPS, FQ, 1, 2, 6, NZ, NXY)
    scale_shape = (GROUPS, FQ, SITES, 2, 1, 1, 1)
    common = jax.random.normal(keys[0], common_shape, jnp.float32)
    own = jax.random.normal(keys[1], shape, jnp.float32)
    spread = jnp.exp(jax.random.uniform(keys[2], scale_shape, jnp.float32, -0.7, 0.7))
    field = jnp.clip(spread * (0.15 * common + own), -8.0, 8.0)
    return field.reshape(GROUPS, 2 * FQ * SITES, 6, NZ, NXY).astype(jnp.bfloat16)


def draw_datum(key, part):
    key = jax.random.fold_in(key, 5)
    total_codes = 4 * FQ * SITES

    def one_group(index):
        group_key = jax.random.fold_in(key, index)
        middle = jax.random.permutation(group_key, total_codes - 2).astype(jnp.int32) + 1
        ends = jnp.array([0, total_codes - 1], jnp.int32)
        chosen = jnp.concatenate([ends, middle[:PANEL - 2]])
        order = jax.random.permutation(jax.random.fold_in(group_key, 1), PANEL)
        return chosen[order]
    return jax.vmap(one_group)(jnp.arange(GROUPS))


def levels(own_key, dims, cuts, least, largest):
    def one(position, blocks):
        draws = jax.random.uniform(jax.random.fold_in(jax.random.fold_in(own_key, 6), position), (blocks,), jnp.float32, least / len(cuts), largest / len(cuts))
        return jnp.repeat(jnp.exp(draws), dims[position] // blocks).reshape((-1,) + (1,) * (len(dims) - position - 1))

    level = one(*cuts[0])
    for cut in cuts[1:]:
        level = level * one(*cut)
    return level


def scatter_about(own_key, shape, scale, limit, cuts=(), held_as=jnp.bfloat16):
    values = jax.random.normal(own_key, shape, jnp.float32) * scale
    if len(cuts) > 0:
        values = levels(own_key, shape, cuts, -0.22, 0.18) * values
    return jnp.clip(values, min=-limit, max=limit).astype(held_as)


def setup_inputs(seed: int = 0) -> dict:
    key_of = jax.random.split(jax.random.key(seed), 5)
    forward = scatter_about(key_of[0], (GROUPS, NF, 6, NZ, NXY), 1.0, 6.0, ((0, 8), (3, 32)))
    adjoint = draw_adjoint(jax.random.fold_in(key_of[4], 71), 0)
    probes = scatter_about(key_of[2], (NZ, NXY, PROBES), (NZ * NXY) ** -0.5, 0.0234375, ((0, 32),))
    datum = draw_datum(jax.random.fold_in(key_of[4], 71), 0)
    return dict(forward=forward, adjoint=adjoint, probes=probes, datum=datum)


def next_column(field, row_length):
    size = field.shape[-1]
    padding = jnp.zeros(field.shape[:-1] + (1,), field.dtype)
    moved = jnp.concatenate([field[..., 1:], padding], axis=-1)
    column = lax.broadcasted_iota(jnp.int32, (size,), 0) % row_length
    return jnp.where(column == row_length - 1, jnp.zeros_like(moved), moved)

def next_row(field, row_length):
    padding = jnp.zeros(field.shape[:-1] + (row_length,), field.dtype)
    return jnp.concatenate([field[..., row_length:], padding], axis=-1)

def edge_product(fwd_pair, adj_pair):
    return fwd_pair[:, 0].astype(jnp.float32) * adj_pair[:, 0].astype(jnp.float32) - fwd_pair[:, 1].astype(jnp.float32) * adj_pair[:, 1].astype(jnp.float32)

def upper_part(fwd_rows, adj_rows, row_length):
    edge_x = edge_product(fwd_rows[:, 0:2], adj_rows[:, 0:2])
    edge_y = edge_product(fwd_rows[:, 2:4], adj_rows[:, 2:4])
    return edge_x + next_row(edge_x, row_length) + edge_y + next_column(edge_y, row_length)

def side_part(fwd_rows, adj_rows, row_length):
    edge_z = edge_product(fwd_rows[:, 0:2], adj_rows[:, 0:2])
    paired = edge_z + next_column(edge_z, row_length)
    return paired + next_row(paired, row_length)

def decode(codes):
    freq_index = codes // (4 * SITES)
    site_index = codes // 4 % SITES
    component = codes % 4
    fwd_index = (freq_index * 2 + component // 2).astype(jnp.int32)
    adj_index = ((freq_index * SITES + site_index) * 2 + component % 2).astype(jnp.int32)
    return (fwd_index, adj_index)

def cholesky_basis(sketch):
    gram = jnp.dot(sketch.T.astype(jnp.float32), sketch.astype(jnp.float32), precision=lax.Precision.HIGHEST, preferred_element_type=jnp.float32)
    factor = jnp.linalg.cholesky(gram)
    solved = lax.linalg.triangular_solve(factor, sketch.T, left_side=True, lower=True)
    return solved.T.astype(jnp.bfloat16)

def reference(forward, adjoint, probes, datum):
    row_length = NX
    probe_flat = probes.reshape(NZ * NXY, PROBES).astype(jnp.float32)
    total = jnp.zeros((PROBES, NZ * NXY), jnp.float32)
    for group in range(GROUPS):
        fwd_index, adj_index = decode(datum[group])
        upper = upper_part(jnp.take(forward[group][:, 0:4], fwd_index, axis=0), jnp.take(adjoint[group][:, 0:4], adj_index, axis=0), row_length)
        upper_next = jnp.concatenate([upper[:, 1:], jnp.zeros((PANEL, 1, NXY), jnp.float32)], axis=1)
        side = side_part(jnp.take(forward[group][:, 4:6], fwd_index, axis=0), jnp.take(adjoint[group][:, 4:6], adj_index, axis=0), row_length)
        sens = (0.25 * (upper + upper_next + side)).astype(jnp.bfloat16)
        sens_wide = lax.optimization_barrier(sens).reshape(PANEL, NZ * NXY).astype(jnp.float32)
        sketch = jnp.dot(sens_wide.astype(jnp.float32), probe_flat.astype(jnp.float32), preferred_element_type=jnp.float32)
        basis = cholesky_basis(sketch)
        for step in range(ITERS):
            basis_wide = lax.optimization_barrier(basis).astype(jnp.float32)
            cells = jnp.dot(basis_wide.T.astype(jnp.float32), sens_wide.astype(jnp.float32), preferred_element_type=jnp.float32).astype(jnp.bfloat16)
            cells_wide = lax.optimization_barrier(cells).astype(jnp.float32)
            sketch = jnp.dot(sens_wide.astype(jnp.float32), cells_wide.T.astype(jnp.float32), preferred_element_type=jnp.float32)
            basis = cholesky_basis(sketch)
        basis_wide = lax.optimization_barrier(basis).astype(jnp.float32)
        total = total + jnp.dot(basis_wide.T.astype(jnp.float32), sens_wide.astype(jnp.float32), preferred_element_type=jnp.float32)
    return total.reshape(PROBES, NZ, NXY)
```

```python
import jax
import jax.numpy as jnp
from jax import lax
from jax.sharding import PartitionSpec as P

SITES = 40
NX = 64
ITERS = 4


def passed_along(block, axis, distance):
    devices = range(lax.axis_size(axis))
    route = [(i - distance, i) for i in devices if i - distance in devices]
    return lax.ppermute(block, axis, route)


def next_column(field, row_length):
    size = field.shape[-1]
    padding = jnp.zeros(field.shape[:-1] + (1,), field.dtype)
    moved = jnp.concatenate([field[..., 1:], padding], axis=-1)
    column = lax.broadcasted_iota(jnp.int32, (size,), 0) % row_length
    return jnp.where(column == row_length - 1, jnp.zeros_like(moved), moved)


def next_row(field, row_length):
    padding = jnp.zeros(field.shape[:-1] + (row_length,), field.dtype)
    return jnp.concatenate([field[..., row_length:], padding], axis=-1)


def edge_product(fwd_pair, adj_pair):
    return fwd_pair[:, 0].astype(jnp.float32) * adj_pair[:, 0].astype(jnp.float32) - fwd_pair[
        :, 1
    ].astype(jnp.float32) * adj_pair[:, 1].astype(jnp.float32)


def upper_part(fwd_rows, adj_rows, row_length):
    edge_x = edge_product(fwd_rows[:, 0:2], adj_rows[:, 0:2])
    edge_y = edge_product(fwd_rows[:, 2:4], adj_rows[:, 2:4])
    return edge_x + next_row(edge_x, row_length) + edge_y + next_column(edge_y, row_length)


def side_part(fwd_rows, adj_rows, row_length):
    edge_z = edge_product(fwd_rows, adj_rows)
    paired = edge_z + next_column(edge_z, row_length)
    return paired + next_row(paired, row_length)


def decode(codes):
    freq_index = codes // (4 * SITES)
    site_index = codes // 4 % SITES
    component = codes % 4
    fwd_index = freq_index * 2 + component // 2
    adj_index = (freq_index * SITES + site_index) * 2 + component % 2
    return (fwd_index, adj_index)


def cholesky_basis(sketch):
    gram = jnp.dot(
        sketch.T, sketch, precision=lax.Precision.HIGHEST, preferred_element_type=jnp.float32
    )
    factor = jnp.linalg.cholesky(gram)
    solved = lax.linalg.triangular_solve(factor, sketch.T, left_side=True, lower=True)
    return solved.T


def brick_moves(step):
    devices = lax.axis_size("brick")
    return [(i, step(i)) for i in range(devices)]


def coordinates(index):
    return index // 8, index // 2 % 4, index % 2


def along_x(k):
    return brick_moves(lambda i: (i + 8 * k) % 32)


def along_z(k):
    return brick_moves(lambda i: i // 8 * 8 + (i % 8 + 2 * k) % 8)


def across_cores():
    return brick_moves(lambda i: i ^ 1)


def pick(parts, index):
    return lax.dynamic_index_in_dim(parts, index, 0, keepdims=False)


def scattered_sum(parts, place, moves):
    count = len(moves) + 1
    got = [lax.ppermute(pick(parts, (place + k) % count), "brick", moves[k - 1]) for k in range(1, count)]
    total = pick(parts, place)
    for part in got:
        total = total + part
    return total


def gathered(part, place, moves):
    count = len(moves) + 1
    got = [part] + [lax.ppermute(part, "brick", move) for move in moves]
    back = jnp.stack((got[::-1] + got[::-1]))
    return lax.dynamic_slice_in_dim(back, (count - 1 - place) % count, count, 0)


def brick_sum(table):
    x, z, core = coordinates(lax.axis_index("brick"))
    x_moves = [along_x(k) for k in (1, 2, 3)]
    part = scattered_sum(table.reshape(2, -1, 128), core, [across_cores()])
    part = scattered_sum(part.reshape(4, -1, 128), x, x_moves)
    got = [part] + [lax.ppermute(part, "brick", along_z(k)) for k in (1, 2, 3)]
    ring = jnp.stack(got[::-1] + got[::-1])
    ring = lax.dynamic_slice_in_dim(ring, (3 - z) % 4, 4, 0)
    part = (ring[0] + ring[1]) + (ring[2] + ring[3])
    part = gathered(part, x, x_moves).reshape(-1, 128)
    return gathered(part, core, [across_cores()]).reshape(table.shape)


def local(forward, adjoint, probes, datum):
    row_length = NX
    fields_fwd = forward[0]
    fields_adj = adjoint[0]
    fwd_index, adj_index = decode(datum[0])
    upper = upper_part(
        jnp.take(fields_fwd[:, 0:4], fwd_index, axis=0),
        jnp.take(fields_adj[:, 0:4], adj_index, axis=0),
        row_length,
    )
    above = passed_along(upper[:, 0, :], "brick", -1)
    upper_next = jnp.concatenate([upper[:, 1:], above[:, None, :]], axis=1)
    side = side_part(
        jnp.take(fields_fwd[:, 4:6], fwd_index, axis=0),
        jnp.take(fields_adj[:, 4:6], adj_index, axis=0),
        row_length,
    )
    sens = (0.25 * (upper + upper_next + side)).astype(jnp.bfloat16)
    sketch = jnp.einsum("pzn,znk->pk", sens, probes, preferred_element_type=jnp.float32)
    cross = jnp.einsum("pzn,qzn->pq", sens, sens, preferred_element_type=jnp.float32)
    table = jnp.concatenate([sketch, cross[:128, :128], cross[:128, 128:], cross[128:, 128:]], axis=0)
    table = brick_sum(table)
    sketch = table[:256]
    top, corner, low = table[256:384], table[384:512], table[512:640]
    cross = jnp.concatenate(
        [jnp.concatenate([top, corner], axis=1), jnp.concatenate([corner.T, low], axis=1)], axis=0
    )
    basis = cholesky_basis(sketch)
    for step in range(ITERS):
        sketch = jnp.dot(
            cross, basis, precision=lax.Precision.HIGHEST, preferred_element_type=jnp.float32
        )
        basis = cholesky_basis(sketch)
    parts = jnp.einsum(
        "pk,pzn->kzn", basis.astype(jnp.bfloat16), sens, preferred_element_type=jnp.float32
    )
    parts = parts.reshape(8, 16, 2, 1024).astype(jnp.bfloat16)
    parts = lax.all_to_all(parts, "freq", 0, 0)
    return parts.astype(jnp.float32).sum(0)


def solution(mesh):
    return jax.shard_map(
        local,
        mesh=mesh,
        in_specs=(
            P("freq", None, None, "brick", None),
            P("freq", None, None, "brick", None),
            P("brick", None, None),
            P("freq", None),
        ),
        out_specs=P("freq", "brick", None),
        check_vma=False,
    )
```

```python
import jax
import jax.numpy as jnp
from jax import lax
from jax.experimental import pallas as pl
from jax.experimental.pallas import tpu as pltpu
from jax.sharding import PartitionSpec as P

SITES = 40
NX = 64
ITERS = 4
PANEL = 256
PROBES = 128
SUB, LANES = 8, 128
BLOCK = 64

WHOLE = pl.BlockSpec(memory_space=pltpu.VMEM)
SCALARS = pl.BlockSpec(memory_space=pltpu.SMEM)
PARAMS = pltpu.CompilerParams(vmem_limit_bytes=40 * 1024 * 1024)


def cost(flops, size):
    return pl.CostEstimate(flops=flops, bytes_accessed=size, transcendentals=0)


def tiled(rows):
    lead = rows.shape[1:3]
    split = rows.reshape(lead + (2, SUB, LANES))
    return jnp.transpose(split, (0, 1, 3, 2, 4)).reshape(lead + (2 * SUB, LANES))


def decode(code):
    second = (code >= 4 * SITES).astype(jnp.int32)
    rest = code - second * (4 * SITES)
    fwd_row = second * 2 + (rest & 3) // 2
    adj_row = second * (2 * SITES) + rest // 4 * 2 + (rest & 1)
    return fwd_row, adj_row


def position(axis):
    return lax.broadcasted_iota(jnp.int32, (2 * SUB, LANES), axis)


def next_column(field):
    return jnp.where(position(1) % NX == NX - 1, 0.0, pltpu.roll(field, LANES - 1, 1))


def next_row(field):
    swapped = pltpu.roll(field, NX, 1)
    later = jnp.where(position(0) >= 2 * SUB - 2, 0.0, pltpu.roll(swapped, 2 * SUB - 2, 0))
    return jnp.where(position(1) < NX, swapped, later)


def edge_product(fwd, adj, fwd_row, adj_row, orientation):
    real, imag = 2 * orientation, 2 * orientation + 1

    def wide(ref, row, part):
        return ref[row, part].astype(jnp.float32)

    return wide(fwd, fwd_row, real) * wide(adj, adj_row, real) - wide(fwd, fwd_row, imag) * wide(
        adj, adj_row, imag
    )


def tile_rows(index, size):
    return pl.ds(pl.multiple_of(index * size, size), size)


def layer_rows(table, block, s, layer):
    return [
        table[pl.ds(block * 256 + half * 128 + 2 * s + layer, SUB, stride=2 * SUB), :]
        for half in range(2)
    ]


def upper_kernel(codes, fwd, adj, upper, lowest):
    def one(d, carry):
        rows = decode(codes[d])
        edge_x = edge_product(fwd, adj, *rows, 0)
        edge_y = edge_product(fwd, adj, *rows, 1)
        upper[tile_rows(d, 16), :] = edge_x + next_row(edge_x) + edge_y + next_column(edge_y)
        return carry

    lax.fori_loop(0, PANEL, one, 0, unroll=8)

    def block(i, carry):
        for s in range(SUB):
            low = jnp.concatenate(layer_rows(upper, i, s, 0), axis=0)
            lowest[s, tile_rows(i, 16), :] = low.astype(jnp.bfloat16)
        return carry

    lax.fori_loop(0, PANEL // 16, block, 0)


def side_kernel(codes, fwd, adj, upper, sens, rest, summed):
    def one(d, carry):
        edge_z = edge_product(fwd, adj, *decode(codes[d]), 0)
        paired = edge_z + next_column(edge_z)
        here = upper[tile_rows(d, 16), :]
        above = jnp.where(position(0) % 2 == 0, pltpu.roll(here, 2 * SUB - 1, 0), 0.0)
        summed[tile_rows(d, 16), :] = here + above + (paired + next_row(paired))
        return carry

    lax.fori_loop(0, PANEL, one, 0, unroll=8)

    def block(i, carry):
        for s in range(SUB):
            low = jnp.concatenate(layer_rows(summed, i, s, 0), axis=0)
            sens[s, tile_rows(i, 16), :] = (0.25 * low).astype(jnp.bfloat16)
            high = layer_rows(summed, i, s, 1)
            rest[s, tile_rows(2 * i, SUB), :] = high[0]
            rest[s, tile_rows(2 * i + 1, SUB), :] = high[1]
        return carry

    lax.fori_loop(0, PANEL // 16, block, 0)


def dot(left, right, left_dim, right_dim, precision=None):
    return lax.dot_general(
        left,
        right,
        (((left_dim,), (right_dim,)), ((), ())),
        precision=precision,
        preferred_element_type=jnp.float32,
    )


def layer_sums(sens, probes, layer):
    cross, sketch = 0.0, 0.0
    for s in range(0, SUB, 2):
        pair = jnp.concatenate([sens[s], sens[s + 1]], axis=1)
        cross = cross + dot(pair, pair, 1, 1)
        sketch = sketch + dot(probes[layer, 128 * s : 128 * s + 256, :], pair, 0, 1)
    return [cross[:128, :128], cross[:128, 128:], cross[128:, 128:], sketch[:, :128], sketch[:, 128:]]


def low_sums_kernel(sens, probes, table):
    for i, part in enumerate(layer_sums(sens, probes, 0)):
        table[128 * i : 128 * i + 128, :] = part


def high_sums_kernel(rest, above, probes, low_table, sens, table):
    def block(i, carry):
        for s in range(SUB):
            here = (s, tile_rows(i, 16), slice(None))
            sens[here] = (0.25 * (rest[here] + above[here].astype(jnp.float32))).astype(jnp.bfloat16)
        return carry

    lax.fori_loop(0, PANEL // 16, block, 0)
    for i, part in enumerate(layer_sums(sens, probes, 1)):
        at = slice(128 * i, 128 * i + 128)
        table[at, :] = low_table[at, :] + part


def spread(column):
    return jnp.broadcast_to(column, (SUB, LANES))


def eliminate(work):
    row = lax.broadcasted_iota(jnp.int32, (SUB, LANES), 0)
    groups = BLOCK // SUB
    for start in range(0, PROBES, BLOCK):
        m = [
            [work[start + SUB * g : start + SUB * g + SUB, h * 128 : h * 128 + 128] for h in range(2)]
            for g in range(groups)
        ]
        for g in range(groups):
            at = start + SUB * g
            column = {
                (q, k): spread(m[q][0][:, at + k : at + k + 1])
                for q in range(g, groups)
                for k in range(SUB)
            }
            u = {(i, k): spread(column[g, k][i : i + 1, :]) for k in range(SUB) for i in range(k + 1)}
            root = []
            for k in range(SUB):
                root.append(lax.rsqrt(u[k, k]))
                for j in range(k + 1, SUB):
                    u[k, j] = u[k, j] * root[k]
                for j in range(k + 1, SUB):
                    for i in range(k + 1, j + 1):
                        u[i, j] = u[i, j] - u[k, i] * u[k, j]
            lead = [[spread(m[g][h][k : k + 1, :]) for h in range(2)] for k in range(SUB)]
            for k in range(SUB):
                for h in range(2):
                    for j in range(k):
                        lead[k][h] = lead[k][h] - u[j, k] * lead[j][h]
                    lead[k][h] = lead[k][h] * root[k]
            for h in range(2):
                m[g][h] = lead[0][h]
                for k in range(1, SUB):
                    m[g][h] = jnp.where(row == k, lead[k][h], m[g][h])
            for q in range(g + 1, groups):
                low = []
                for k in range(SUB):
                    entry = column[q, k]
                    for j in range(k):
                        entry = entry - low[j] * u[j, k]
                    low.append(entry * root[k])
                for h in range(2):
                    for k in range(SUB):
                        m[q][h] = m[q][h] - low[k] * lead[k][h]
        for g in range(groups):
            for h in range(2):
                work[start + SUB * g : start + SUB * g + SUB, h * 128 : h * 128 + 128] = m[g][h]
        if start + BLOCK < PROBES:
            done = work[start : start + BLOCK, :]
            change = dot(done[:, :PROBES], done, 0, 0, lax.Precision.HIGHEST)
            work[start + BLOCK :, :] = work[start + BLOCK :, :] - change[start + BLOCK :, :]


def basis_kernel(table, sens_low, sens_high, parts, work, sketch, cross):
    highest = lax.Precision.HIGHEST
    corner = table[128:256, :]
    cross[0:128, 0:128] = table[0:128, :]
    cross[0:128, 128:256] = corner
    cross[128:256, 0:128] = corner.T
    cross[128:256, 128:256] = table[256:384, :]
    sketch[:, 0:128] = table[384:512, :]
    sketch[:, 128:256] = table[512:640, :]
    identity = jnp.where(
        lax.broadcasted_iota(jnp.int32, (PROBES, PROBES), 0)
        == lax.broadcasted_iota(jnp.int32, (PROBES, PROBES), 1),
        1.0,
        0.0,
    )

    def orthonormalize(step, carry):
        rows = sketch[...]
        work[:, 0:128] = dot(rows, rows, 1, 1, highest)
        work[:, 128:256] = identity
        eliminate(work)

        @pl.when(step < ITERS)
        def _():
            moved = dot(sketch[...], cross[...], 1, 0, highest)
            sketch[...] = dot(work[:, 128:256], moved, 1, 0, highest)

        return carry

    lax.fori_loop(0, ITERS + 1, orthonormalize, 0)
    basis = dot(work[:, 128:256], sketch[...], 1, 0, highest).astype(jnp.bfloat16)
    for layer, sens in enumerate((sens_low, sens_high)):
        for s in range(SUB):
            at = 1024 * layer + 128 * s
            parts[:, at : at + 128] = dot(basis, sens[s], 1, 0).astype(jnp.bfloat16)


def brick_moves(step):
    devices = lax.axis_size("brick")
    return [(i, step(i)) for i in range(devices)]


def coordinates(index):
    return index // 8, index // 2 % 4, index % 2


def along_x(k):
    return brick_moves(lambda i: (i + 8 * k) % 32)


def along_z(k):
    return brick_moves(lambda i: i // 8 * 8 + (i % 8 + 2 * k) % 8)


def across_cores():
    return brick_moves(lambda i: i ^ 1)


def pick(parts, index):
    return lax.dynamic_index_in_dim(parts, index, 0, keepdims=False)


def scattered_sum(parts, place, moves):
    count = len(moves) + 1
    got = [lax.ppermute(pick(parts, (place + k) % count), "brick", moves[k - 1]) for k in range(1, count)]
    total = pick(parts, place)
    for part in got:
        total = total + part
    return total


def gathered(part, place, moves):
    count = len(moves) + 1
    got = [part] + [lax.ppermute(part, "brick", move) for move in moves]
    back = jnp.stack((got[::-1] + got[::-1]))
    return lax.dynamic_slice_in_dim(back, (count - 1 - place) % count, count, 0)


def brick_sum(table):
    x, z, core = coordinates(lax.axis_index("brick"))
    x_moves = [along_x(k) for k in (1, 2, 3)]
    part = scattered_sum(table.reshape(2, -1, 128), core, [across_cores()])
    part = scattered_sum(part.reshape(4, -1, 128), x, x_moves)
    got = [part] + [lax.ppermute(part, "brick", along_z(k)) for k in (1, 2, 3)]
    ring = jnp.stack(got[::-1] + got[::-1])
    ring = lax.dynamic_slice_in_dim(ring, (3 - z) % 4, 4, 0)
    part = (ring[0] + ring[1]) + (ring[2] + ring[3])
    part = gathered(part, x, x_moves).reshape(-1, 128)
    return gathered(part, core, [across_cores()]).reshape(table.shape)


def shape(*dims, dtype=jnp.float32):
    return jax.ShapeDtypeStruct(dims, dtype)


def field_rows(count, parts, at):
    return pl.BlockSpec((count, parts, 16, LANES), lambda i: (0, at, 0, 0))


def whole(*dims):
    return pl.BlockSpec(dims, lambda i: (0,) * len(dims))


def local(forward, adjoint, probes, datum):
    fwd, adj, codes = tiled(forward), tiled(adjoint), datum[0]
    layer = (SUB, PANEL, LANES)
    upper, lowest = pl.pallas_call(
        upper_kernel,
        grid=(1,),
        in_specs=[SCALARS, field_rows(4, 4, 0), field_rows(160, 4, 0)],
        out_specs=(whole(PANEL * 16, LANES), whole(*layer)),
        out_shape=(shape(PANEL * 16, LANES), shape(*layer, dtype=jnp.bfloat16)),
        compiler_params=PARAMS,
        cost_estimate=cost(20_000_000, 6_000_000),
        name="upper",
    )(codes, fwd, adj)
    devices = range(lax.axis_size("brick"))
    above = lax.ppermute(lowest, "brick", [(i + 1, i) for i in devices if i + 1 in devices])
    sens_low, rest = pl.pallas_call(
        side_kernel,
        grid=(1,),
        in_specs=[SCALARS, field_rows(4, 2, 2), field_rows(160, 2, 2), whole(PANEL * 16, LANES)],
        out_specs=(whole(*layer), whole(*layer)),
        out_shape=(shape(*layer, dtype=jnp.bfloat16), shape(*layer)),
        scratch_shapes=[pltpu.VMEM((PANEL * 16, LANES), jnp.float32)],
        compiler_params=PARAMS,
        cost_estimate=cost(20_000_000, 30_000_000),
        name="side",
    )(codes, fwd, adj, upper)
    low_table = pl.pallas_call(
        low_sums_kernel,
        in_specs=[WHOLE] * 2,
        out_specs=WHOLE,
        out_shape=shape(640, 128),
        compiler_params=PARAMS,
        cost_estimate=cost(200_000_000, 3_000_000),
        name="low_sums",
    )(sens_low, probes)
    sens_high, table = pl.pallas_call(
        high_sums_kernel,
        in_specs=[WHOLE] * 4,
        out_specs=(WHOLE, WHOLE),
        out_shape=(shape(*layer, dtype=jnp.bfloat16), shape(640, 128)),
        compiler_params=PARAMS,
        cost_estimate=cost(200_000_000, 3_000_000),
        name="high_sums",
    )(rest, above, probes, low_table)
    table = brick_sum(table)
    parts = pl.pallas_call(
        basis_kernel,
        in_specs=[WHOLE] * 3,
        out_specs=WHOLE,
        out_shape=shape(PROBES, 2048, dtype=jnp.bfloat16),
        scratch_shapes=[
            pltpu.VMEM((PROBES, 2 * PROBES), jnp.float32),
            pltpu.VMEM((PROBES, PANEL), jnp.float32),
            pltpu.VMEM((PANEL, PANEL), jnp.float32),
        ],
        compiler_params=PARAMS,
        cost_estimate=cost(400_000_000, 60_000_000),
        name="basis",
    )(table, sens_low, sens_high)
    parts = lax.all_to_all(parts.reshape(8, 16, 2048), "freq", 0, 0)
    return parts.astype(jnp.float32).sum(0).reshape(16, 2, 1024)


def solution(mesh):
    return jax.shard_map(
        local,
        mesh=mesh,
        in_specs=(
            P("freq", None, None, "brick", None),
            P("freq", None, None, "brick", None),
            P("brick", None, None),
            P("freq", None),
        ),
        out_specs=P("freq", "brick", None),
        check_vma=False,
    )
```

```python
import jax
import jax.numpy as jnp
from jax import lax
from jax.experimental import pallas as pl
from jax.experimental.pallas import tpu as pltpu
from jax.sharding import PartitionSpec as P

SITES = 40
NX = 64
ITERS = 4
PANEL = 256
PROBES = 128
SUB, LANES = 8, 128
BLOCK = 64

WHOLE = pl.BlockSpec(memory_space=pltpu.VMEM)
SCALARS = pl.BlockSpec(memory_space=pltpu.SMEM)
PARAMS = pltpu.CompilerParams(vmem_limit_bytes=40 * 1024 * 1024)


def cost(flops, size):
    return pl.CostEstimate(flops=flops, bytes_accessed=size, transcendentals=0)


def tiled(rows):
    lead = rows.shape[1:3]
    split = rows.reshape(lead + (2, SUB, LANES))
    return jnp.transpose(split, (0, 1, 3, 2, 4)).reshape(lead + (2 * SUB, LANES))


def decode(code):
    second = (code >= 4 * SITES).astype(jnp.int32)
    rest = code - second * (4 * SITES)
    fwd_row = second * 2 + (rest & 3) // 2
    adj_row = second * (2 * SITES) + rest // 4 * 2 + (rest & 1)
    return fwd_row, adj_row


def position(axis):
    return lax.broadcasted_iota(jnp.int32, (SUB, LANES), axis)


def next_column(field):
    return jnp.where(position(1) % NX == NX - 1, 0.0, pltpu.roll(field, LANES - 1, 1))


def next_row(field):
    swapped = pltpu.roll(field, NX, 1)
    later = jnp.where(position(0) == SUB - 1, 0.0, pltpu.roll(swapped, SUB - 1, 0))
    return jnp.where(position(1) < NX, swapped, later)


def tile_rows(index, size):
    return pl.ds(pl.multiple_of(index * size, size), size)


def widen(narrow, wide, start, count, parts):
    def one(i, carry):
        for k in range(parts):
            wide[tile_rows(i * parts + k, 16), :] = narrow[i, k].astype(jnp.float32)
        return carry

    lax.fori_loop(start, start + count, one, 0, unroll=4)


def load_rows(parts, codes, fwd, adj, scratch):
    rows, row_table, fwd_narrow, adj_narrow, fwd_wide, adj_wide, done = scratch
    half = adj.shape[0] // 2
    low, high = slice(0, half), slice(half, 2 * half)
    copies = [
        pltpu.make_async_copy(adj.at[low, 0:parts], adj_narrow.at[low], done.at[0]),
        pltpu.make_async_copy(fwd.at[:, 0:parts], fwd_narrow, done.at[1]),
        pltpu.make_async_copy(adj.at[high, 0:parts], adj_narrow.at[high], done.at[2]),
    ]
    for copy in copies:
        copy.start()
    row_table[0:1, :], row_table[1:2, :] = decode(codes[...])
    table_copy = pltpu.make_async_copy(row_table, rows, done.at[3])
    table_copy.start()
    copies[1].wait()
    widen(fwd_narrow, fwd_wide, 0, fwd.shape[0], parts)
    copies[0].wait()
    widen(adj_narrow, adj_wide, 0, half, parts)
    copies[2].wait()
    widen(adj_narrow, adj_wide, half, half, parts)
    table_copy.wait()

    def product(d, orientation, layer):
        def field(wide, row, part):
            return wide[pl.ds(row * (parts * 16) + part * 16 + layer, SUB, stride=2), :]

        fwd_row, adj_row = rows[0, d], rows[1, d]
        real, imag = 2 * orientation, 2 * orientation + 1
        return field(fwd_wide, fwd_row, real) * field(adj_wide, adj_row, real) - field(
            fwd_wide, fwd_row, imag
        ) * field(adj_wide, adj_row, imag)

    return product


def row_scratch(parts):
    return [
        pltpu.SMEM((SUB, PANEL), jnp.int32),
        pltpu.VMEM((SUB, PANEL), jnp.int32),
        pltpu.VMEM((4, parts, 16, LANES), jnp.bfloat16),
        pltpu.VMEM((160, parts, 16, LANES), jnp.bfloat16),
        pltpu.VMEM((4 * parts * 16, LANES), jnp.float32),
        pltpu.VMEM((160 * parts * 16, LANES), jnp.float32),
        pltpu.SemaphoreType.DMA((4,)),
    ]


def chunk(table, block, s):
    return [table[pl.ds(block * 128 + half * 64 + s, SUB, stride=SUB), :] for half in range(2)]


def upper_kernel(codes, fwd, adj, low_upper, lowest, *scratch):
    product = load_rows(4, codes, fwd, adj, scratch)

    def one(d, carry):
        edge_x, edge_y = product(d, 0, 0), product(d, 1, 0)
        low_upper[tile_rows(d, SUB), :] = edge_x + next_row(edge_x) + (edge_y + next_column(edge_y))
        return carry

    lax.fori_loop(0, PANEL, one, 0, unroll=32)

    def block(i, carry):
        for s in range(SUB):
            piece = jnp.concatenate(chunk(low_upper, i, s), axis=0)
            lowest[s, tile_rows(i, 16), :] = piece.astype(jnp.bfloat16)
        return carry

    lax.fori_loop(0, PANEL // 16, block, 0, unroll=2)


def side_kernel(codes, fwd, adj, low_upper, sens, rest, low, high, *scratch):
    product = load_rows(6, codes, fwd, adj, scratch)

    def one(d, carry):
        edge_x, edge_y = product(d, 0, 1), product(d, 1, 1)
        edge_z = [product(d, 2, layer) for layer in range(2)]
        across = edge_y + next_column(edge_y)
        down = [edge_x + (edge + next_column(edge)) for edge in edge_z]
        here = tile_rows(d, SUB)
        low[here, :] = low_upper[here, :] + (across + (down[0] + next_row(down[0])))
        high[here, :] = across + (down[1] + next_row(down[1]))
        return carry

    lax.fori_loop(0, PANEL, one, 0, unroll=16)

    def block(i, carry):
        for s in range(SUB):
            piece = jnp.concatenate(chunk(low, i, s), axis=0)
            sens[s, tile_rows(i, 16), :] = (0.25 * piece).astype(jnp.bfloat16)
            pieces = chunk(high, i, s)
            rest[s, tile_rows(2 * i, SUB), :] = pieces[0]
            rest[s, tile_rows(2 * i + 1, SUB), :] = pieces[1]
        return carry

    lax.fori_loop(0, PANEL // 16, block, 0, unroll=2)


def dot(left, right, left_dim, right_dim, precision=None):
    return lax.dot_general(
        left,
        right,
        (((left_dim,), (right_dim,)), ((), ())),
        precision=precision,
        preferred_element_type=jnp.float32,
    )


def layer_sums(sens, probes, layer):
    cross, sketch = 0.0, 0.0
    for s in range(0, SUB, 2):
        pair = jnp.concatenate([sens[s], sens[s + 1]], axis=1)
        cross = cross + dot(pair, pair, 1, 1)
        sketch = sketch + dot(probes[layer, 128 * s : 128 * s + 256, :], pair, 0, 1)
    return [cross[:128, :128], cross[:128, 128:], cross[128:, 128:], sketch[:, :128], sketch[:, 128:]]


def low_sums_kernel(sens, probes, table):
    for i, part in enumerate(layer_sums(sens, probes, 0)):
        table[128 * i : 128 * i + 128, :] = part


def high_sums_kernel(rest, above, probes, low_table, sens, table):
    def block(i, carry):
        for s in range(SUB):
            here = (s, tile_rows(i, 16), slice(None))
            sens[here] = (0.25 * (rest[here] + above[here].astype(jnp.float32))).astype(jnp.bfloat16)
        return carry

    lax.fori_loop(0, PANEL // 16, block, 0)
    for i, part in enumerate(layer_sums(sens, probes, 1)):
        at = slice(128 * i, 128 * i + 128)
        table[at, :] = low_table[at, :] + part


def spread(column):
    return jnp.broadcast_to(column, (SUB, LANES))


def eliminate(work):
    row = lax.broadcasted_iota(jnp.int32, (SUB, LANES), 0)
    groups = BLOCK // SUB
    for start in range(0, PROBES, BLOCK):
        m = [
            [work[start + SUB * g : start + SUB * g + SUB, h * 128 : h * 128 + 128] for h in range(2)]
            for g in range(groups)
        ]
        for g in range(groups):
            at = start + SUB * g
            column = {
                (q, k): spread(m[q][0][:, at + k : at + k + 1])
                for q in range(g, groups)
                for k in range(SUB)
            }
            u = {(i, k): spread(column[g, k][i : i + 1, :]) for k in range(SUB) for i in range(k + 1)}
            root = []
            for k in range(SUB):
                root.append(lax.rsqrt(u[k, k]))
                for j in range(k + 1, SUB):
                    u[k, j] = u[k, j] * root[k]
                for j in range(k + 1, SUB):
                    for i in range(k + 1, j + 1):
                        u[i, j] = u[i, j] - u[k, i] * u[k, j]
            lead = [[spread(m[g][h][k : k + 1, :]) for h in range(2)] for k in range(SUB)]
            for k in range(SUB):
                for h in range(2):
                    for j in range(k):
                        lead[k][h] = lead[k][h] - u[j, k] * lead[j][h]
                    lead[k][h] = lead[k][h] * root[k]
            for h in range(2):
                m[g][h] = lead[0][h]
                for k in range(1, SUB):
                    m[g][h] = jnp.where(row == k, lead[k][h], m[g][h])
            for q in range(g + 1, groups):
                low = []
                for k in range(SUB):
                    entry = column[q, k]
                    for j in range(k):
                        entry = entry - low[j] * u[j, k]
                    low.append(entry * root[k])
                for h in range(2):
                    for k in range(SUB):
                        m[q][h] = m[q][h] - low[k] * lead[k][h]
        for g in range(groups):
            for h in range(2):
                work[start + SUB * g : start + SUB * g + SUB, h * 128 : h * 128 + 128] = m[g][h]
        if start + BLOCK < PROBES:
            done = work[start : start + BLOCK, :]
            change = dot(done[:, :PROBES], done, 0, 0, lax.Precision.HIGHEST)
            work[start + BLOCK :, :] = work[start + BLOCK :, :] - change[start + BLOCK :, :]


def basis_kernel(table, sens_low, sens_high, parts, work, sketch, cross):
    highest = lax.Precision.HIGHEST
    corner = table[128:256, :]
    cross[0:128, 0:128] = table[0:128, :]
    cross[0:128, 128:256] = corner
    cross[128:256, 0:128] = corner.T
    cross[128:256, 128:256] = table[256:384, :]
    sketch[:, 0:128] = table[384:512, :]
    sketch[:, 128:256] = table[512:640, :]
    identity = jnp.where(
        lax.broadcasted_iota(jnp.int32, (PROBES, PROBES), 0)
        == lax.broadcasted_iota(jnp.int32, (PROBES, PROBES), 1),
        1.0,
        0.0,
    )

    def orthonormalize(step, carry):
        rows = sketch[...]
        work[:, 0:128] = dot(rows, rows, 1, 1, highest)
        work[:, 128:256] = identity
        eliminate(work)

        @pl.when(step < ITERS)
        def _():
            moved = dot(sketch[...], cross[...], 1, 0, highest)
            sketch[...] = dot(work[:, 128:256], moved, 1, 0, highest)

        return carry

    lax.fori_loop(0, ITERS + 1, orthonormalize, 0)
    basis = dot(work[:, 128:256], sketch[...], 1, 0, highest).astype(jnp.bfloat16)
    for layer, sens in enumerate((sens_low, sens_high)):
        for s in range(SUB):
            at = 1024 * layer + 128 * s
            parts[:, at : at + 128] = dot(basis, sens[s], 1, 0).astype(jnp.bfloat16)


def brick_moves(step):
    devices = lax.axis_size("brick")
    return [(i, step(i)) for i in range(devices)]


def coordinates(index):
    return index // 8, index // 2 % 4, index % 2


def along_x(k):
    return brick_moves(lambda i: (i + 8 * k) % 32)


def along_z(k):
    return brick_moves(lambda i: i // 8 * 8 + (i % 8 + 2 * k) % 8)


def across_cores():
    return brick_moves(lambda i: i ^ 1)


def pick(parts, index):
    return lax.dynamic_index_in_dim(parts, index, 0, keepdims=False)


def scattered_sum(parts, place, moves):
    count = len(moves) + 1
    got = [lax.ppermute(pick(parts, (place + k) % count), "brick", moves[k - 1]) for k in range(1, count)]
    total = pick(parts, place)
    for part in got:
        total = total + part
    return total


def gathered(part, place, moves):
    count = len(moves) + 1
    got = [part] + [lax.ppermute(part, "brick", move) for move in moves]
    back = jnp.stack((got[::-1] + got[::-1]))
    return lax.dynamic_slice_in_dim(back, (count - 1 - place) % count, count, 0)


def brick_sum(table):
    x, z, core = coordinates(lax.axis_index("brick"))
    x_moves = [along_x(k) for k in (1, 2, 3)]
    part = scattered_sum(table.reshape(2, -1, 128), core, [across_cores()])
    part = scattered_sum(part.reshape(4, -1, 128), x, x_moves)
    got = [part] + [lax.ppermute(part, "brick", along_z(k)) for k in (1, 2, 3)]
    ring = jnp.stack(got[::-1] + got[::-1])
    ring = lax.dynamic_slice_in_dim(ring, (3 - z) % 4, 4, 0)
    part = (ring[0] + ring[1]) + (ring[2] + ring[3])
    part = gathered(part, x, x_moves).reshape(-1, 128)
    return gathered(part, core, [across_cores()]).reshape(table.shape)


def shape(*dims, dtype=jnp.float32):
    return jax.ShapeDtypeStruct(dims, dtype)


def local(forward, adjoint, probes, datum):
    fwd, adj = tiled(forward), tiled(adjoint)
    layer = (SUB, PANEL, LANES)
    anywhere = pl.BlockSpec(memory_space=pl.ANY)
    low_upper, lowest = pl.pallas_call(
        upper_kernel,
        in_specs=[WHOLE, anywhere, anywhere],
        out_specs=(WHOLE, WHOLE),
        out_shape=(shape(PANEL * SUB, LANES), shape(*layer, dtype=jnp.bfloat16)),
        scratch_shapes=row_scratch(4),
        compiler_params=pltpu.CompilerParams(vmem_limit_bytes=60 * 1024 * 1024),
        cost_estimate=cost(10_000_000, 8_000_000),
        name="upper",
    )(datum, fwd, adj)
    devices = range(lax.axis_size("brick"))
    above = lax.ppermute(lowest, "brick", [(i + 1, i) for i in devices if i + 1 in devices])
    sens_low, rest = pl.pallas_call(
        side_kernel,
        in_specs=[WHOLE, anywhere, anywhere, WHOLE],
        out_specs=(WHOLE, WHOLE),
        out_shape=(shape(*layer, dtype=jnp.bfloat16), shape(*layer)),
        scratch_shapes=[pltpu.VMEM((PANEL * SUB, LANES), jnp.float32)] * 2 + row_scratch(6),
        compiler_params=PARAMS,
        cost_estimate=cost(20_000_000, 30_000_000),
        name="side",
    )(datum, fwd, adj, low_upper)
    low_table = pl.pallas_call(
        low_sums_kernel,
        in_specs=[WHOLE] * 2,
        out_specs=WHOLE,
        out_shape=shape(640, 128),
        compiler_params=PARAMS,
        cost_estimate=cost(200_000_000, 3_000_000),
        name="low_sums",
    )(sens_low, probes)
    sens_high, table = pl.pallas_call(
        high_sums_kernel,
        in_specs=[WHOLE] * 4,
        out_specs=(WHOLE, WHOLE),
        out_shape=(shape(*layer, dtype=jnp.bfloat16), shape(640, 128)),
        compiler_params=PARAMS,
        cost_estimate=cost(200_000_000, 3_000_000),
        name="high_sums",
    )(rest, above, probes, low_table)
    table = brick_sum(table)
    parts = pl.pallas_call(
        basis_kernel,
        in_specs=[WHOLE] * 3,
        out_specs=WHOLE,
        out_shape=shape(PROBES, 2048, dtype=jnp.bfloat16),
        scratch_shapes=[
            pltpu.VMEM((PROBES, 2 * PROBES), jnp.float32),
            pltpu.VMEM((PROBES, PANEL), jnp.float32),
            pltpu.VMEM((PANEL, PANEL), jnp.float32),
        ],
        compiler_params=PARAMS,
        cost_estimate=cost(400_000_000, 60_000_000),
        name="basis",
    )(table, sens_low, sens_high)
    parts = lax.all_to_all(parts.reshape(8, 16, 2048), "freq", 0, 0)
    return parts.astype(jnp.float32).sum(0).reshape(16, 2, 1024)


def solution(mesh):
    return jax.shard_map(
        local,
        mesh=mesh,
        in_specs=(
            P("freq", None, None, "brick", None),
            P("freq", None, None, "brick", None),
            P("brick", None, None),
            P("freq", None),
        ),
        out_specs=P("freq", "brick", None),
        check_vma=False,
    )
```

```python
import jax
import jax.numpy as jnp
from jax import lax
from jax.experimental import pallas as pl
from jax.experimental.pallas import tpu as pltpu
from jax.sharding import PartitionSpec as P

SITES = 40
NX = 64
ITERS = 4
PANEL = 256
PROBES = 128
SUB, LANES = 8, 128
HALF = 64

WHOLE = pl.BlockSpec(memory_space=pltpu.VMEM)
SCALARS = pl.BlockSpec(memory_space=pltpu.SMEM)
PARAMS = pltpu.CompilerParams(vmem_limit_bytes=40 * 1024 * 1024)


def cost(flops, size):
    return pl.CostEstimate(flops=flops, bytes_accessed=size, transcendentals=0)


def tiled(rows):
    lead = rows.shape[1:3]
    split = rows.reshape(lead + (2, SUB, LANES))
    return jnp.transpose(split, (0, 1, 3, 2, 4)).reshape(lead + (2 * SUB, LANES))


def decode(code):
    second = (code >= 4 * SITES).astype(jnp.int32)
    rest = code - second * (4 * SITES)
    fwd_row = second * 2 + (rest & 3) // 2
    adj_row = second * (2 * SITES) + rest // 4 * 2 + (rest & 1)
    return fwd_row, adj_row


def position(axis):
    return lax.broadcasted_iota(jnp.int32, (SUB, LANES), axis)


def next_column(field):
    return jnp.where(position(1) % NX == NX - 1, 0.0, pltpu.roll(field, LANES - 1, 1))


def next_row(field):
    swapped = pltpu.roll(field, NX, 1)
    later = jnp.where(position(0) == SUB - 1, 0.0, pltpu.roll(swapped, SUB - 1, 0))
    return jnp.where(position(1) < NX, swapped, later)


def tile_rows(index, size):
    return pl.ds(pl.multiple_of(index * size, size), size)


def widen(narrow, wide, start, count, parts):
    def one(i, carry):
        for k in range(parts):
            wide[tile_rows(i * parts + k, 16), :] = narrow[i, k].astype(jnp.float32)
        return carry

    lax.fori_loop(start, start + count, one, 0, unroll=4)


def load_rows(parts, codes, fwd, adj, scratch):
    rows, row_table, fwd_narrow, adj_narrow, fwd_wide, adj_wide, done = scratch
    half = adj.shape[0] // 2
    low, high = slice(0, half), slice(half, 2 * half)
    copies = [
        pltpu.make_async_copy(adj.at[low, 0:parts], adj_narrow.at[low], done.at[0]),
        pltpu.make_async_copy(fwd.at[:, 0:parts], fwd_narrow, done.at[1]),
        pltpu.make_async_copy(adj.at[high, 0:parts], adj_narrow.at[high], done.at[2]),
    ]
    for copy in copies:
        copy.start()
    row_table[0:1, :], row_table[1:2, :] = decode(codes[...])
    table_copy = pltpu.make_async_copy(row_table, rows, done.at[3])
    table_copy.start()
    copies[1].wait()
    widen(fwd_narrow, fwd_wide, 0, fwd.shape[0], parts)
    copies[0].wait()
    widen(adj_narrow, adj_wide, 0, half, parts)
    copies[2].wait()
    widen(adj_narrow, adj_wide, half, half, parts)
    table_copy.wait()

    def product(d, orientation, layer):
        def field(wide, row, part):
            return wide[pl.ds(row * (parts * 16) + part * 16 + layer, SUB, stride=2), :]

        fwd_row, adj_row = rows[0, d], rows[1, d]
        real, imag = 2 * orientation, 2 * orientation + 1
        return field(fwd_wide, fwd_row, real) * field(adj_wide, adj_row, real) - field(
            fwd_wide, fwd_row, imag
        ) * field(adj_wide, adj_row, imag)

    return product


def row_scratch(parts):
    return [
        pltpu.SMEM((SUB, PANEL), jnp.int32),
        pltpu.VMEM((SUB, PANEL), jnp.int32),
        pltpu.VMEM((4, parts, 16, LANES), jnp.bfloat16),
        pltpu.VMEM((160, parts, 16, LANES), jnp.bfloat16),
        pltpu.VMEM((4 * parts * 16, LANES), jnp.float32),
        pltpu.VMEM((160 * parts * 16, LANES), jnp.float32),
        pltpu.SemaphoreType.DMA((4,)),
    ]


def chunk(table, block, s):
    return [table[pl.ds(block * 128 + half * 64 + s, SUB, stride=SUB), :] for half in range(2)]


def upper_kernel(codes, fwd, adj, low_upper, lowest, *scratch):
    product = load_rows(4, codes, fwd, adj, scratch)

    def one(d, carry):
        edge_x, edge_y = product(d, 0, 0), product(d, 1, 0)
        low_upper[tile_rows(d, SUB), :] = edge_x + next_row(edge_x) + (edge_y + next_column(edge_y))
        return carry

    lax.fori_loop(0, PANEL, one, 0, unroll=32)

    def block(i, carry):
        for s in range(SUB):
            piece = jnp.concatenate(chunk(low_upper, i, s), axis=0)
            lowest[s, tile_rows(i, 16), :] = piece.astype(jnp.bfloat16)
        return carry

    lax.fori_loop(0, PANEL // 16, block, 0, unroll=2)


def side_kernel(codes, fwd, adj, low_upper, sens, rest, low, high, *scratch):
    product = load_rows(6, codes, fwd, adj, scratch)

    def one(d, carry):
        edge_x, edge_y = product(d, 0, 1), product(d, 1, 1)
        edge_z = [product(d, 2, layer) for layer in range(2)]
        across = edge_y + next_column(edge_y)
        down = [edge_x + (edge + next_column(edge)) for edge in edge_z]
        here = tile_rows(d, SUB)
        low[here, :] = low_upper[here, :] + (across + (down[0] + next_row(down[0])))
        high[here, :] = across + (down[1] + next_row(down[1]))
        return carry

    lax.fori_loop(0, PANEL, one, 0, unroll=16)

    def block(i, carry):
        for s in range(SUB):
            piece = jnp.concatenate(chunk(low, i, s), axis=0)
            sens[s, tile_rows(i, 16), :] = (0.25 * piece).astype(jnp.bfloat16)
            pieces = chunk(high, i, s)
            rest[s, tile_rows(2 * i, SUB), :] = pieces[0]
            rest[s, tile_rows(2 * i + 1, SUB), :] = pieces[1]
        return carry

    lax.fori_loop(0, PANEL // 16, block, 0, unroll=2)


def dot(left, right, left_dim, right_dim, precision=None):
    return lax.dot_general(
        left,
        right,
        (((left_dim,), (right_dim,)), ((), ())),
        precision=precision,
        preferred_element_type=jnp.float32,
    )


def layer_sums(sens, probes, layer):
    cross, sketch = 0.0, 0.0
    for s in range(0, SUB, 2):
        pair = jnp.concatenate([sens[s], sens[s + 1]], axis=1)
        cross = cross + dot(pair, pair, 1, 1)
        sketch = sketch + dot(probes[layer, 128 * s : 128 * s + 256, :], pair, 0, 1)
    return [cross[:128, :128], cross[:128, 128:], cross[128:, 128:], sketch[:, :128], sketch[:, 128:]]


def low_sums_kernel(sens, probes, table):
    for i, part in enumerate(layer_sums(sens, probes, 0)):
        table[128 * i : 128 * i + 128, :] = part


def high_sums_kernel(rest, above, probes, low_table, sens, table):
    def block(i, carry):
        for s in range(SUB):
            here = (s, tile_rows(i, 16), slice(None))
            sens[here] = (0.25 * (rest[here] + above[here].astype(jnp.float32))).astype(jnp.bfloat16)
        return carry

    lax.fori_loop(0, PANEL // 16, block, 0)
    for i, part in enumerate(layer_sums(sens, probes, 1)):
        at = slice(128 * i, 128 * i + 128)
        table[at, :] = low_table[at, :] + part


def spread(piece):
    return jnp.broadcast_to(piece, (SUB, LANES))


def column_of_each(piece, at):
    left = lax.broadcasted_iota(jnp.int32, (SUB, LANES), 1) < HALF
    return jnp.where(left, spread(piece[:, at : at + 1]), spread(piece[:, HALF + at : HALF + at + 1]))


def eliminate_panel(gram, inverse, g):
    row = lax.broadcasted_iota(jnp.int32, (SUB, LANES), 0)
    later = range(g + 1, len(gram))
    column = {
        (q, k): column_of_each(gram[q], SUB * g + k) for q in (g, *later) for k in range(SUB)
    }
    u = {(i, k): spread(column[g, k][i : i + 1, :]) for k in range(SUB) for i in range(k + 1)}
    root = []
    for k in range(SUB):
        root.append(lax.rsqrt(u[k, k]))
        for j in range(k + 1, SUB):
            u[k, j] = u[k, j] * root[k]
        for j in range(k + 1, SUB):
            for i in range(k + 1, j + 1):
                u[i, j] = u[i, j] - u[k, i] * u[k, j]
    low = {}
    for q in later:
        for k in range(SUB):
            entry = column[q, k]
            for j in range(k):
                entry = entry - low[q, j] * u[j, k]
            low[q, k] = entry * root[k]
    for table in (gram, inverse):
        lead = [spread(table[g][k : k + 1, :]) for k in range(SUB)]
        for k in range(SUB):
            for j in range(k):
                lead[k] = lead[k] - u[j, k] * lead[j]
            lead[k] = lead[k] * root[k]
        table[g] = lead[0]
        for k in range(1, SUB):
            table[g] = jnp.where(row == k, lead[k], table[g])
        for q in later:
            for k in range(SUB):
                table[q] = table[q] - low[q, k] * lead[k]


def exact_dot(left, right, left_dim, right_dim):
    return dot(left, right, left_dim, right_dim, lax.Precision.HIGHEST)


def padded(block, side):
    zeros = jnp.zeros_like(block)
    return jnp.concatenate([zeros, block] if side else [block, zeros], axis=0)


def basis_kernel(table, sens_low, sens_high, parts, basis, sketch, cross):
    corner = table[128:256, :]
    cross[0:128, 0:128] = table[0:128, :]
    cross[0:128, 128:256] = corner
    cross[128:256, 0:128] = corner.T
    cross[128:256, 128:256] = table[256:384, :]
    sketch[0, :, 0:128] = table[384:512, :]
    sketch[0, :, 128:256] = table[512:640, :]
    identity = jnp.where(
        lax.broadcasted_iota(jnp.int32, (HALF, LANES), 0)
        == lax.broadcasted_iota(jnp.int32, (HALF, LANES), 1) % HALF,
        1.0,
        0.0,
    )
    halves = (slice(0, HALF), slice(HALF, PROBES))
    for wave in range(ITERS + 2):
        work = [(half, wave - half) for half in (0, 1) if 0 <= wave - half <= ITERS]
        gram, rows = 0.0, []
        for half, stage in work:
            sides = (half,) if len(work) == 2 else (0, 1)
            x = sketch[stage, halves[half], :]
            for side in sides:
                gram = gram + exact_dot(x, padded(x, side), 1, 1)
            if half == 1:
                before = basis[stage, halves[0], :]
                overlap = exact_dot(x, before, 1, 1)
                for side in sides:
                    gram = gram - exact_dot(overlap, padded(overlap, side), 1, 1)
                x = x - exact_dot(overlap, before, 1, 0)
            rows.append(x)
        moved = exact_dot(jnp.concatenate(rows, axis=0), cross[...], 1, 0)
        gram_rows = [gram[SUB * g : SUB * g + SUB, :] for g in range(HALF // SUB)]
        inverse_rows = [identity[SUB * g : SUB * g + SUB, :] for g in range(HALF // SUB)]
        for g in range(HALF // SUB):
            eliminate_panel(gram_rows, inverse_rows, g)
        inverse = jnp.concatenate(inverse_rows, axis=0)
        for at, (half, stage) in enumerate(work):
            both = jnp.concatenate([rows[at], moved[HALF * at : HALF * at + HALF, :]], axis=1)
            done = exact_dot(inverse[:, halves[half]], both, 1, 0)
            basis[stage, halves[half], :] = done[:, :PANEL]
            if stage < ITERS:
                sketch[stage + 1, halves[half], :] = done[:, PANEL:]
    final = basis[ITERS].astype(jnp.bfloat16)
    for layer, sens in enumerate((sens_low, sens_high)):
        for s in range(SUB):
            at = 1024 * layer + 128 * s
            parts[:, at : at + 128] = dot(final, sens[s], 1, 0).astype(jnp.bfloat16)


def brick_moves(step):
    devices = lax.axis_size("brick")
    return [(i, step(i)) for i in range(devices)]


def coordinates(index):
    return index // 8, index // 2 % 4, index % 2


def along_x(k):
    return brick_moves(lambda i: (i + 8 * k) % 32)


def along_z(k):
    return brick_moves(lambda i: i // 8 * 8 + (i % 8 + 2 * k) % 8)


def across_cores():
    return brick_moves(lambda i: i ^ 1)


def pick(parts, index):
    return lax.dynamic_index_in_dim(parts, index, 0, keepdims=False)


def scattered_sum(parts, place, moves):
    count = len(moves) + 1
    got = [lax.ppermute(pick(parts, (place + k) % count), "brick", moves[k - 1]) for k in range(1, count)]
    total = pick(parts, place)
    for part in got:
        total = total + part
    return total


def gathered(part, place, moves):
    count = len(moves) + 1
    got = [part] + [lax.ppermute(part, "brick", move) for move in moves]
    back = jnp.stack((got[::-1] + got[::-1]))
    return lax.dynamic_slice_in_dim(back, (count - 1 - place) % count, count, 0)


def brick_sum(table):
    x, z, core = coordinates(lax.axis_index("brick"))
    x_moves = [along_x(k) for k in (1, 2, 3)]
    part = scattered_sum(table.reshape(2, -1, 128), core, [across_cores()])
    part = scattered_sum(part.reshape(4, -1, 128), x, x_moves)
    got = [part] + [lax.ppermute(part, "brick", along_z(k)) for k in (1, 2, 3)]
    ring = jnp.stack(got[::-1] + got[::-1])
    ring = lax.dynamic_slice_in_dim(ring, (3 - z) % 4, 4, 0)
    part = (ring[0] + ring[1]) + (ring[2] + ring[3])
    part = gathered(part, x, x_moves).reshape(-1, 128)
    return gathered(part, core, [across_cores()]).reshape(table.shape)


def shape(*dims, dtype=jnp.float32):
    return jax.ShapeDtypeStruct(dims, dtype)


def local(forward, adjoint, probes, datum):
    fwd, adj = tiled(forward), tiled(adjoint)
    layer = (SUB, PANEL, LANES)
    anywhere = pl.BlockSpec(memory_space=pl.ANY)
    low_upper, lowest = pl.pallas_call(
        upper_kernel,
        in_specs=[WHOLE, anywhere, anywhere],
        out_specs=(WHOLE, WHOLE),
        out_shape=(shape(PANEL * SUB, LANES), shape(*layer, dtype=jnp.bfloat16)),
        scratch_shapes=row_scratch(4),
        compiler_params=pltpu.CompilerParams(vmem_limit_bytes=60 * 1024 * 1024),
        cost_estimate=cost(10_000_000, 8_000_000),
        name="upper",
    )(datum, fwd, adj)
    devices = range(lax.axis_size("brick"))
    above = lax.ppermute(lowest, "brick", [(i + 1, i) for i in devices if i + 1 in devices])
    sens_low, rest = pl.pallas_call(
        side_kernel,
        in_specs=[WHOLE, anywhere, anywhere, WHOLE],
        out_specs=(WHOLE, WHOLE),
        out_shape=(shape(*layer, dtype=jnp.bfloat16), shape(*layer)),
        scratch_shapes=[pltpu.VMEM((PANEL * SUB, LANES), jnp.float32)] * 2 + row_scratch(6),
        compiler_params=PARAMS,
        cost_estimate=cost(20_000_000, 30_000_000),
        name="side",
    )(datum, fwd, adj, low_upper)
    low_table = pl.pallas_call(
        low_sums_kernel,
        in_specs=[WHOLE] * 2,
        out_specs=WHOLE,
        out_shape=shape(640, 128),
        compiler_params=PARAMS,
        cost_estimate=cost(200_000_000, 3_000_000),
        name="low_sums",
    )(sens_low, probes)
    sens_high, table = pl.pallas_call(
        high_sums_kernel,
        in_specs=[WHOLE] * 4,
        out_specs=(WHOLE, WHOLE),
        out_shape=(shape(*layer, dtype=jnp.bfloat16), shape(640, 128)),
        compiler_params=PARAMS,
        cost_estimate=cost(200_000_000, 3_000_000),
        name="high_sums",
    )(rest, above, probes, low_table)
    table = brick_sum(table)
    parts = pl.pallas_call(
        basis_kernel,
        in_specs=[WHOLE] * 3,
        out_specs=WHOLE,
        out_shape=shape(PROBES, 2048, dtype=jnp.bfloat16),
        scratch_shapes=[
            pltpu.VMEM((ITERS + 1, PROBES, PANEL), jnp.float32),
            pltpu.VMEM((ITERS + 1, PROBES, PANEL), jnp.float32),
            pltpu.VMEM((PANEL, PANEL), jnp.float32),
        ],
        compiler_params=PARAMS,
        cost_estimate=cost(400_000_000, 60_000_000),
        name="basis",
    )(table, sens_low, sens_high)
    parts = lax.all_to_all(parts.reshape(8, 16, 2048), "freq", 0, 0)
    return parts.astype(jnp.float32).sum(0).reshape(16, 2, 1024)


def solution(mesh):
    return jax.shard_map(
        local,
        mesh=mesh,
        in_specs=(
            P("freq", None, None, "brick", None),
            P("freq", None, None, "brick", None),
            P("brick", None, None),
            P("freq", None),
        ),
        out_specs=P("freq", "brick", None),
        check_vma=False,
    )
```

```python
import jax
import jax.numpy as jnp
from jax import lax
from jax.experimental import pallas as pl
from jax.experimental.pallas import tpu as pltpu
from jax.sharding import PartitionSpec as P

SITES = 40
NX = 64
ITERS = 4
PANEL = 256
PROBES = 128
SUB, LANES = 8, 128
HALF = 64

WHOLE = pl.BlockSpec(memory_space=pltpu.VMEM)
SCALARS = pl.BlockSpec(memory_space=pltpu.SMEM)
PARAMS = pltpu.CompilerParams(vmem_limit_bytes=40 * 1024 * 1024)


def cost(flops, size):
    return pl.CostEstimate(flops=flops, bytes_accessed=size, transcendentals=0)


def tiled(rows):
    lead = rows.shape[1:3]
    split = rows.reshape(lead + (2, SUB, LANES))
    return jnp.transpose(split, (0, 1, 3, 2, 4)).reshape(lead + (2 * SUB, LANES))


def decode(code):
    second = (code >= 4 * SITES).astype(jnp.int32)
    rest = code - second * (4 * SITES)
    fwd_row = second * 2 + (rest & 3) // 2
    adj_row = second * (2 * SITES) + rest // 4 * 2 + (rest & 1)
    return fwd_row, adj_row


def position(axis):
    return lax.broadcasted_iota(jnp.int32, (SUB, LANES), axis)


def next_column(field):
    return jnp.where(position(1) % NX == NX - 1, 0.0, pltpu.roll(field, LANES - 1, 1))


def next_row(field):
    swapped = pltpu.roll(field, NX, 1)
    later = jnp.where(position(0) == SUB - 1, 0.0, pltpu.roll(swapped, SUB - 1, 0))
    return jnp.where(position(1) < NX, swapped, later)


def tile_rows(index, size):
    return pl.ds(pl.multiple_of(index * size, size), size)


def widen(narrow, wide, start, count, parts):
    def one(i, carry):
        for k in range(parts):
            wide[tile_rows(i * parts + k, 16), :] = narrow[i, k].astype(jnp.float32)
        return carry

    lax.fori_loop(start, start + count, one, 0, unroll=4)


def load_rows(parts, codes, fwd, adj, scratch):
    rows, row_table, fwd_narrow, adj_narrow, fwd_wide, adj_wide, done = scratch
    half = adj.shape[0] // 2
    low, high = slice(0, half), slice(half, 2 * half)
    copies = [
        pltpu.make_async_copy(adj.at[low, 0:parts], adj_narrow.at[low], done.at[0]),
        pltpu.make_async_copy(fwd.at[:, 0:parts], fwd_narrow, done.at[1]),
        pltpu.make_async_copy(adj.at[high, 0:parts], adj_narrow.at[high], done.at[2]),
    ]
    for copy in copies:
        copy.start()
    row_table[0:1, :], row_table[1:2, :] = decode(codes[...])
    table_copy = pltpu.make_async_copy(row_table, rows, done.at[3])
    table_copy.start()
    copies[1].wait()
    widen(fwd_narrow, fwd_wide, 0, fwd.shape[0], parts)
    copies[0].wait()
    widen(adj_narrow, adj_wide, 0, half, parts)
    copies[2].wait()
    widen(adj_narrow, adj_wide, half, half, parts)
    table_copy.wait()

    def product(d, orientation, layer):
        def field(wide, row, part):
            return wide[pl.ds(row * (parts * 16) + part * 16 + layer, SUB, stride=2), :]

        fwd_row, adj_row = rows[0, d], rows[1, d]
        real, imag = 2 * orientation, 2 * orientation + 1
        return field(fwd_wide, fwd_row, real) * field(adj_wide, adj_row, real) - field(
            fwd_wide, fwd_row, imag
        ) * field(adj_wide, adj_row, imag)

    return product


def row_scratch(parts):
    return [
        pltpu.SMEM((SUB, PANEL), jnp.int32),
        pltpu.VMEM((SUB, PANEL), jnp.int32),
        pltpu.VMEM((4, parts, 16, LANES), jnp.bfloat16),
        pltpu.VMEM((160, parts, 16, LANES), jnp.bfloat16),
        pltpu.VMEM((4 * parts * 16, LANES), jnp.float32),
        pltpu.VMEM((160 * parts * 16, LANES), jnp.float32),
        pltpu.SemaphoreType.DMA((4,)),
    ]


def chunk(table, block, s):
    return [table[pl.ds(block * 128 + half * 64 + s, SUB, stride=SUB), :] for half in range(2)]


def upper_kernel(codes, fwd, adj, low_upper, lowest, *scratch):
    product = load_rows(4, codes, fwd, adj, scratch)

    def one(d, carry):
        edge_x, edge_y = product(d, 0, 0), product(d, 1, 0)
        low_upper[tile_rows(d, SUB), :] = edge_x + next_row(edge_x) + (edge_y + next_column(edge_y))
        return carry

    lax.fori_loop(0, PANEL, one, 0, unroll=64)

    def block(i, carry):
        for s in range(SUB):
            piece = jnp.concatenate(chunk(low_upper, i, s), axis=0)
            lowest[s, tile_rows(i, 16), :] = piece.astype(jnp.bfloat16)
        return carry

    lax.fori_loop(0, PANEL // 16, block, 0, unroll=2)


def side_kernel(codes, fwd, adj, low_upper, sens, rest, low, high, *scratch):
    product = load_rows(6, codes, fwd, adj, scratch)

    def one(d, carry):
        edge_x, edge_y = product(d, 0, 1), product(d, 1, 1)
        edge_z = [product(d, 2, layer) for layer in range(2)]
        across = edge_y + next_column(edge_y)
        down = [edge_x + (edge + next_column(edge)) for edge in edge_z]
        here = tile_rows(d, SUB)
        low[here, :] = low_upper[here, :] + (across + (down[0] + next_row(down[0])))
        high[here, :] = across + (down[1] + next_row(down[1]))
        return carry

    lax.fori_loop(0, PANEL, one, 0, unroll=16)

    def block(i, carry):
        for s in range(SUB):
            piece = jnp.concatenate(chunk(low, i, s), axis=0)
            sens[s, tile_rows(i, 16), :] = (0.25 * piece).astype(jnp.bfloat16)
            pieces = chunk(high, i, s)
            rest[s, tile_rows(2 * i, SUB), :] = pieces[0]
            rest[s, tile_rows(2 * i + 1, SUB), :] = pieces[1]
        return carry

    lax.fori_loop(0, PANEL // 16, block, 0, unroll=2)


def dot(left, right, left_dim, right_dim, precision=None):
    return lax.dot_general(
        left,
        right,
        (((left_dim,), (right_dim,)), ((), ())),
        precision=precision,
        preferred_element_type=jnp.float32,
    )


def layer_sums(sens, probes, layer):
    cross, sketch = 0.0, 0.0
    for s in range(0, SUB, 2):
        pair = jnp.concatenate([sens[s], sens[s + 1]], axis=1)
        cross = cross + dot(pair, pair, 1, 1)
        sketch = sketch + dot(probes[layer, 128 * s : 128 * s + 256, :], pair, 0, 1)
    return cross, sketch


def block_index(axis):
    return lax.broadcasted_iota(jnp.int32, (LANES, LANES), axis)


def low_sums_kernel(sens, probes, cross, sketch):
    cross[...], sketch[...] = layer_sums(sens, probes, 0)


def high_sums_kernel(rest, above, probes, low_cross, low_sketch, sens, table):
    def block(i, carry):
        for s in range(SUB):
            here = (s, tile_rows(i, 16), slice(None))
            sens[here] = (0.25 * (rest[here] + above[here].astype(jnp.float32))).astype(jnp.bfloat16)
        return carry

    lax.fori_loop(0, PANEL // 16, block, 0)
    cross, sketch = layer_sums(sens, probes, 1)
    cross, sketch = cross + low_cross[...], sketch + low_sketch[...]
    table[0:128, :], table[128:256, :] = sketch[:, :128], sketch[:, 128:]
    table[256:384, :] = cross[:128, 128:]
    last = cross[128:, 128:]
    table[384:512, :] = jnp.where(block_index(0) <= block_index(1), cross[:128, :128], last)
    diagonal = jnp.sum(jnp.where(block_index(0) == block_index(1), last, 0.0), axis=0, keepdims=True)
    table[512:544, :] = jnp.broadcast_to(diagonal, (32, LANES))


def spread(piece):
    return jnp.broadcast_to(piece, (SUB, LANES))


def column_of_each(piece, at):
    left = lax.broadcasted_iota(jnp.int32, (SUB, LANES), 1) < HALF
    return jnp.where(left, spread(piece[:, at : at + 1]), spread(piece[:, HALF + at : HALF + at + 1]))


def own_columns(gram, g):
    return [column_of_each(gram[g], SUB * g + k) for k in range(SUB)]


def eliminate_panel(gram, inverse, g, own):
    row = lax.broadcasted_iota(jnp.int32, (SUB, LANES), 0)
    later = range(g + 1, len(gram))
    column = {(q, k): column_of_each(gram[q], SUB * g + k) for q in later for k in range(SUB)}
    following = own_columns(gram, g + 1) if later else None
    u = {(i, k): spread(own[k][i : i + 1, :]) for k in range(SUB) for i in range(k + 1)}
    root = []
    for k in range(SUB):
        root.append(lax.rsqrt(u[k, k]))
        for j in range(k + 1, SUB):
            u[k, j] = u[k, j] * root[k]
        for j in range(k + 1, SUB):
            for i in range(k + 1, j + 1):
                u[i, j] = u[i, j] - u[k, i] * u[k, j]
    low = {}
    for q in later:
        for k in range(SUB):
            entry = column[q, k]
            for j in range(k):
                entry = entry - low[q, j] * u[j, k]
            low[q, k] = entry * root[k]
    if later:
        for c in range(SUB):
            for k in range(SUB):
                across = low[g + 1, k]
                following[c] = following[c] - across * spread(across[c : c + 1, :])
    for table in (gram, inverse):
        lead = [spread(table[g][k : k + 1, :]) for k in range(SUB)]
        for k in range(SUB):
            for j in range(k):
                lead[k] = lead[k] - u[j, k] * lead[j]
            lead[k] = lead[k] * root[k]
        table[g] = lead[0]
        for k in range(1, SUB):
            table[g] = jnp.where(row == k, lead[k], table[g])
        for q in later:
            for k in range(SUB):
                table[q] = table[q] - low[q, k] * lead[k]
    return following


def exact_dot(left, right, left_dim, right_dim):
    return dot(left, right, left_dim, right_dim, lax.Precision.HIGHEST)


def padded(block, side):
    zeros = jnp.zeros_like(block)
    return jnp.concatenate([zeros, block] if side else [block, zeros], axis=0)


def basis_kernel(table, sens_low, sens_high, parts, basis, sketch, cross):
    sketch[0, :, 0:128], sketch[0, :, 128:256] = table[0:128, :], table[128:256, :]
    corner, packed = table[256:384, :], table[384:512, :]
    turned = packed.T
    row, column = block_index(0), block_index(1)
    cross[0:128, 0:128] = jnp.where(row <= column, packed, turned)
    cross[0:128, 128:256] = corner
    cross[128:256, 0:128] = corner.T
    last = jnp.where(row > column, packed, turned)
    cross[128:256, 128:256] = jnp.where(row == column, table[512:513, :], last)
    identity = jnp.where(
        lax.broadcasted_iota(jnp.int32, (HALF, LANES), 0)
        == lax.broadcasted_iota(jnp.int32, (HALF, LANES), 1) % HALF,
        1.0,
        0.0,
    )
    halves = (slice(0, HALF), slice(HALF, PROBES))
    for wave in range(ITERS + 2):
        work = [(half, wave - half) for half in (0, 1) if 0 <= wave - half <= ITERS]
        gram, rows = 0.0, []
        for half, stage in work:
            sides = (half,) if len(work) == 2 else (0, 1)
            x = sketch[stage, halves[half], :]
            for side in sides:
                gram = gram + exact_dot(x, padded(x, side), 1, 1)
            if half == 1:
                before = basis[stage, halves[0], :]
                overlap = exact_dot(x, before, 1, 1)
                for side in sides:
                    gram = gram - exact_dot(overlap, padded(overlap, side), 1, 1)
                x = x - exact_dot(overlap, before, 1, 0)
            rows.append(x)
        moved = exact_dot(jnp.concatenate(rows, axis=0), cross[...], 1, 0)
        gram_rows = [gram[SUB * g : SUB * g + SUB, :] for g in range(HALF // SUB)]
        inverse_rows = [identity[SUB * g : SUB * g + SUB, :] for g in range(HALF // SUB)]
        own = own_columns(gram_rows, 0)
        for g in range(HALF // SUB):
            own = eliminate_panel(gram_rows, inverse_rows, g, own)
        inverse = jnp.concatenate(inverse_rows, axis=0)
        for at, (half, stage) in enumerate(work):
            both = jnp.concatenate([rows[at], moved[HALF * at : HALF * at + HALF, :]], axis=1)
            done = exact_dot(inverse[:, halves[half]], both, 1, 0)
            basis[stage, halves[half], :] = done[:, :PANEL]
            if stage < ITERS:
                sketch[stage + 1, halves[half], :] = done[:, PANEL:]
    final = basis[ITERS].astype(jnp.bfloat16)
    for layer, sens in enumerate((sens_low, sens_high)):
        for s in range(SUB):
            at = 1024 * layer + 128 * s
            parts[:, at : at + 128] = dot(final, sens[s], 1, 0).astype(jnp.bfloat16)


def brick_moves(step):
    devices = lax.axis_size("brick")
    return [(i, step(i)) for i in range(devices)]


def coordinates(index):
    return index // 8, index // 2 % 4, index % 2


def across_cores():
    return brick_moves(lambda i: i ^ 1)


def pick(parts, index):
    return lax.dynamic_index_in_dim(parts, index, 0, keepdims=False)


def pairs(i, step):
    return i ^ 1 if step == 0 else 3 - i


def pair_x(step):
    return brick_moves(lambda i: pairs(i // 8, step) * 8 + i % 8)


def pair_z(step):
    return brick_moves(lambda i: i // 8 * 8 + pairs(i % 8 // 2, step) * 2 + i % 2)


def halved(table, keep, move):
    parts = table.reshape(2, -1, 128)
    return pick(parts, keep) + lax.ppermute(pick(parts, 1 - keep), "brick", move)


def doubled(part, kept, move):
    other = lax.ppermute(part, "brick", move)
    return jnp.where(kept == 0, jnp.concatenate([part, other]), jnp.concatenate([other, part]))


def brick_sum(table):
    x, _, core = coordinates(lax.axis_index("brick"))
    inner = ((x == 1) | (x == 2)).astype(jnp.int32)
    part = halved(table, core, across_cores())
    part = halved(part, inner, pair_x(0))
    part = part + lax.ppermute(part, "brick", pair_x(1))
    part = part + lax.ppermute(part, "brick", pair_z(0))
    part = part + lax.ppermute(part, "brick", pair_z(1))
    part = doubled(part, inner, pair_x(0))
    return doubled(part, core, across_cores())


def shape(*dims, dtype=jnp.float32):
    return jax.ShapeDtypeStruct(dims, dtype)


def local(forward, adjoint, probes, datum):
    fwd, adj = tiled(forward), tiled(adjoint)
    layer = (SUB, PANEL, LANES)
    anywhere = pl.BlockSpec(memory_space=pl.ANY)
    low_upper, lowest = pl.pallas_call(
        upper_kernel,
        in_specs=[WHOLE, anywhere, anywhere],
        out_specs=(WHOLE, WHOLE),
        out_shape=(shape(PANEL * SUB, LANES), shape(*layer, dtype=jnp.bfloat16)),
        scratch_shapes=row_scratch(4),
        compiler_params=pltpu.CompilerParams(vmem_limit_bytes=60 * 1024 * 1024),
        cost_estimate=cost(10_000_000, 8_000_000),
        name="upper",
    )(datum, fwd, adj)
    devices = range(lax.axis_size("brick"))
    above = lax.ppermute(lowest, "brick", [(i + 1, i) for i in devices if i + 1 in devices])
    sens_low, rest = pl.pallas_call(
        side_kernel,
        in_specs=[WHOLE, anywhere, anywhere, WHOLE],
        out_specs=(WHOLE, WHOLE),
        out_shape=(shape(*layer, dtype=jnp.bfloat16), shape(*layer)),
        scratch_shapes=[pltpu.VMEM((PANEL * SUB, LANES), jnp.float32)] * 2 + row_scratch(6),
        compiler_params=PARAMS,
        cost_estimate=cost(20_000_000, 30_000_000),
        name="side",
    )(datum, fwd, adj, low_upper)
    low_cross, low_sketch = pl.pallas_call(
        low_sums_kernel,
        in_specs=[WHOLE] * 2,
        out_specs=(WHOLE, WHOLE),
        out_shape=(shape(PANEL, PANEL), shape(PROBES, PANEL)),
        compiler_params=PARAMS,
        cost_estimate=cost(200_000_000, 3_000_000),
        name="low_sums",
    )(sens_low, probes)
    sens_high, table = pl.pallas_call(
        high_sums_kernel,
        in_specs=[WHOLE] * 5,
        out_specs=(WHOLE, WHOLE),
        out_shape=(shape(*layer, dtype=jnp.bfloat16), shape(544, 128)),
        compiler_params=PARAMS,
        cost_estimate=cost(200_000_000, 3_000_000),
        name="high_sums",
    )(rest, above, probes, low_cross, low_sketch)
    table = brick_sum(table)
    parts = pl.pallas_call(
        basis_kernel,
        in_specs=[WHOLE] * 3,
        out_specs=WHOLE,
        out_shape=shape(PROBES, 2048, dtype=jnp.bfloat16),
        scratch_shapes=[
            pltpu.VMEM((ITERS + 1, PROBES, PANEL), jnp.float32),
            pltpu.VMEM((ITERS + 1, PROBES, PANEL), jnp.float32),
            pltpu.VMEM((PANEL, PANEL), jnp.float32),
        ],
        compiler_params=PARAMS,
        cost_estimate=cost(400_000_000, 60_000_000),
        name="basis",
    )(table, sens_low, sens_high)
    parts = lax.all_to_all(parts.reshape(8, 16, 2048), "freq", 0, 0)
    return parts.astype(jnp.float32).sum(0).reshape(16, 2, 1024)


def solution(mesh):
    return jax.shard_map(
        local,
        mesh=mesh,
        in_specs=(
            P("freq", None, None, "brick", None),
            P("freq", None, None, "brick", None),
            P("brick", None, None),
            P("freq", None),
        ),
        out_specs=P("freq", "brick", None),
        check_vma=False,
    )
```

```python
import jax
import jax.numpy as jnp
from jax import lax
from jax.experimental import pallas as pl
from jax.experimental.pallas import tpu as pltpu
from jax.sharding import PartitionSpec as P

SITES = 40
NX = 64
ITERS = 4
PANEL = 256
PROBES = 128
SUB, LANES = 8, 128
HALF = 64

WHOLE = pl.BlockSpec(memory_space=pltpu.VMEM)
SCALARS = pl.BlockSpec(memory_space=pltpu.SMEM)
PARAMS = pltpu.CompilerParams(vmem_limit_bytes=40 * 1024 * 1024)


def cost(flops, size):
    return pl.CostEstimate(flops=flops, bytes_accessed=size, transcendentals=0)


def tiled(rows):
    lead = rows.shape[1:3]
    split = rows.reshape(lead + (2, SUB, LANES))
    return jnp.transpose(split, (0, 1, 3, 2, 4)).reshape(lead + (2 * SUB, LANES))


def decode(code):
    second = (code >= 4 * SITES).astype(jnp.int32)
    rest = code - second * (4 * SITES)
    fwd_row = second * 2 + (rest & 3) // 2
    adj_row = second * (2 * SITES) + rest // 4 * 2 + (rest & 1)
    return fwd_row, adj_row


def position(axis):
    return lax.broadcasted_iota(jnp.int32, (SUB, LANES), axis)


def next_column(field):
    return jnp.where(position(1) % NX == NX - 1, 0.0, pltpu.roll(field, LANES - 1, 1))


def next_row(field):
    swapped = pltpu.roll(field, NX, 1)
    later = jnp.where(position(0) == SUB - 1, 0.0, pltpu.roll(swapped, SUB - 1, 0))
    return jnp.where(position(1) < NX, swapped, later)


def tile_rows(index, size):
    return pl.ds(pl.multiple_of(index * size, size), size)


def widen(narrow, wide, start, count, parts):
    def one(i, carry):
        for k in range(parts):
            wide[tile_rows(i * parts + k, 16), :] = narrow[i, k].astype(jnp.float32)
        return carry

    lax.fori_loop(start, start + count, one, 0, unroll=4)


def load_rows(parts, codes, fwd, adj, scratch):
    rows, row_table, fwd_narrow, adj_narrow, fwd_wide, adj_wide, done = scratch
    half = adj.shape[0] // 2
    low, high = slice(0, half), slice(half, 2 * half)
    copies = [
        pltpu.make_async_copy(adj.at[low, 0:parts], adj_narrow.at[low], done.at[0]),
        pltpu.make_async_copy(fwd.at[:, 0:parts], fwd_narrow, done.at[1]),
        pltpu.make_async_copy(adj.at[high, 0:parts], adj_narrow.at[high], done.at[2]),
    ]
    for copy in copies:
        copy.start()
    row_table[0:1, :], row_table[1:2, :] = decode(codes[...])
    table_copy = pltpu.make_async_copy(row_table, rows, done.at[3])
    table_copy.start()
    copies[1].wait()
    widen(fwd_narrow, fwd_wide, 0, fwd.shape[0], parts)
    copies[0].wait()
    widen(adj_narrow, adj_wide, 0, half, parts)
    copies[2].wait()
    widen(adj_narrow, adj_wide, half, half, parts)
    table_copy.wait()

    def product(d, orientation, layer):
        def field(wide, row, part):
            return wide[pl.ds(row * (parts * 16) + part * 16 + layer, SUB, stride=2), :]

        fwd_row, adj_row = rows[0, d], rows[1, d]
        real, imag = 2 * orientation, 2 * orientation + 1
        return field(fwd_wide, fwd_row, real) * field(adj_wide, adj_row, real) - field(
            fwd_wide, fwd_row, imag
        ) * field(adj_wide, adj_row, imag)

    return product


def row_scratch(parts):
    return [
        pltpu.SMEM((SUB, PANEL), jnp.int32),
        pltpu.VMEM((SUB, PANEL), jnp.int32),
        pltpu.VMEM((4, parts, 16, LANES), jnp.bfloat16),
        pltpu.VMEM((160, parts, 16, LANES), jnp.bfloat16),
        pltpu.VMEM((4 * parts * 16, LANES), jnp.float32),
        pltpu.VMEM((160 * parts * 16, LANES), jnp.float32),
        pltpu.SemaphoreType.DMA((4,)),
    ]


def chunk(table, block, s):
    return [table[pl.ds(block * 128 + half * 64 + s, SUB, stride=SUB), :] for half in range(2)]


def upper_kernel(codes, fwd, adj, lowest, low_upper, *scratch):
    product = load_rows(4, codes, fwd, adj, scratch)

    def one(d, carry):
        edge_x, edge_y = product(d, 0, 0), product(d, 1, 0)
        low_upper[tile_rows(d, SUB), :] = edge_x + next_row(edge_x) + (edge_y + next_column(edge_y))
        return carry

    lax.fori_loop(0, PANEL, one, 0, unroll=64)

    def block(i, carry):
        for s in range(SUB):
            piece = jnp.concatenate(chunk(low_upper, i, s), axis=0)
            lowest[s, tile_rows(i, 16), :] = piece.astype(jnp.bfloat16)
        return carry

    lax.fori_loop(0, PANEL // 16, block, 0, unroll=2)


def side_kernel(codes, fwd, adj, sens, rest, low, high, *scratch):
    product = load_rows(6, codes, fwd, adj, scratch)

    def one(d, carry):
        edge_x, edge_y, edge_z = [
            [product(d, orientation, layer) for layer in range(2)] for orientation in range(3)
        ]
        paired = [edge + next_column(edge) for edge in edge_z]
        across = edge_y[1] + next_column(edge_y[1])
        both = edge_y[0] + next_column(edge_y[0]) + across
        down = [edge_x[0] + edge_x[1] + paired[0], edge_x[1] + paired[1]]
        low[tile_rows(d, SUB), :] = both + (down[0] + next_row(down[0]))
        high[tile_rows(d, SUB), :] = across + (down[1] + next_row(down[1]))
        return carry

    lax.fori_loop(0, PANEL, one, 0, unroll=16)

    def block(i, carry):
        for s in range(SUB):
            piece = jnp.concatenate(chunk(low, i, s), axis=0)
            sens[s, tile_rows(i, 16), :] = (0.25 * piece).astype(jnp.bfloat16)
            pieces = chunk(high, i, s)
            rest[s, tile_rows(2 * i, SUB), :] = pieces[0]
            rest[s, tile_rows(2 * i + 1, SUB), :] = pieces[1]
        return carry

    lax.fori_loop(0, PANEL // 16, block, 0, unroll=2)


def dot(left, right, left_dim, right_dim, precision=None):
    return lax.dot_general(
        left,
        right,
        (((left_dim,), (right_dim,)), ((), ())),
        precision=precision,
        preferred_element_type=jnp.float32,
    )


def layer_sums(sens, probes, layer):
    cross, sketch = 0.0, 0.0
    for s in range(0, SUB, 2):
        pair = jnp.concatenate([sens[s], sens[s + 1]], axis=1)
        cross = cross + dot(pair, pair, 1, 1)
        sketch = sketch + dot(probes[layer, 128 * s : 128 * s + 256, :], pair, 0, 1)
    return cross, sketch


def block_index(axis):
    return lax.broadcasted_iota(jnp.int32, (LANES, LANES), axis)


def low_sums_kernel(sens, probes, cross, sketch):
    cross[...], sketch[...] = layer_sums(sens, probes, 0)


def high_sums_kernel(rest, above, probes, low_cross, low_sketch, sens, table):
    def block(i, carry):
        for s in range(SUB):
            here = (s, tile_rows(i, 16), slice(None))
            sens[here] = (0.25 * (rest[here] + above[here].astype(jnp.float32))).astype(jnp.bfloat16)
        return carry

    lax.fori_loop(0, PANEL // 16, block, 0)
    cross, sketch = layer_sums(sens, probes, 1)
    cross, sketch = cross + low_cross[...], sketch + low_sketch[...]
    table[0:128, :], table[128:256, :] = sketch[:, :128], sketch[:, 128:]
    table[256:384, :] = cross[:128, 128:]
    last = cross[128:, 128:]
    table[384:512, :] = jnp.where(block_index(0) <= block_index(1), cross[:128, :128], last)
    diagonal = jnp.sum(jnp.where(block_index(0) == block_index(1), last, 0.0), axis=0, keepdims=True)
    table[512:544, :] = jnp.broadcast_to(diagonal, (32, LANES))


def spread(piece):
    return jnp.broadcast_to(piece, (SUB, LANES))


def column_of_each(piece, at):
    left = lax.broadcasted_iota(jnp.int32, (SUB, LANES), 1) < HALF
    return jnp.where(left, spread(piece[:, at : at + 1]), spread(piece[:, HALF + at : HALF + at + 1]))


def own_columns(gram, g):
    return [column_of_each(gram[g], SUB * g + k) for k in range(SUB)]


def eliminate_panel(gram, inverse, g, own):
    row = lax.broadcasted_iota(jnp.int32, (SUB, LANES), 0)
    later = range(g + 1, len(gram))
    column = {(q, k): column_of_each(gram[q], SUB * g + k) for q in later for k in range(SUB)}
    following = own_columns(gram, g + 1) if later else None
    u = {(i, k): spread(own[k][i : i + 1, :]) for k in range(SUB) for i in range(k + 1)}
    root = []
    for k in range(SUB):
        root.append(lax.rsqrt(u[k, k]))
        for j in range(k + 1, SUB):
            u[k, j] = u[k, j] * root[k]
        for j in range(k + 1, SUB):
            for i in range(k + 1, j + 1):
                u[i, j] = u[i, j] - u[k, i] * u[k, j]
    low = {}
    for q in later:
        for k in range(SUB):
            entry = column[q, k]
            for j in range(k):
                entry = entry - low[q, j] * u[j, k]
            low[q, k] = entry * root[k]
    if later:
        for c in range(SUB):
            for k in range(SUB):
                across = low[g + 1, k]
                following[c] = following[c] - across * spread(across[c : c + 1, :])
    for table in (gram, inverse):
        lead = [spread(table[g][k : k + 1, :]) for k in range(SUB)]
        for k in range(SUB):
            for j in range(k):
                lead[k] = lead[k] - u[j, k] * lead[j]
            lead[k] = lead[k] * root[k]
        table[g] = lead[0]
        for k in range(1, SUB):
            table[g] = jnp.where(row == k, lead[k], table[g])
        for q in later:
            for k in range(SUB):
                table[q] = table[q] - low[q, k] * lead[k]
    return following


def exact_dot(left, right, left_dim, right_dim):
    return dot(left, right, left_dim, right_dim, lax.Precision.HIGHEST)


def padded(block, side):
    zeros = jnp.zeros_like(block)
    return jnp.concatenate([zeros, block] if side else [block, zeros], axis=0)


def basis_kernel(table, sens_low, sens_high, parts, basis, sketch, cross):
    sketch[0, :, 0:128], sketch[0, :, 128:256] = table[0:128, :], table[128:256, :]
    corner, packed = table[256:384, :], table[384:512, :]
    turned = packed.T
    row, column = block_index(0), block_index(1)
    cross[0:128, 0:128] = jnp.where(row <= column, packed, turned)
    cross[0:128, 128:256] = corner
    cross[128:256, 0:128] = corner.T
    last = jnp.where(row > column, packed, turned)
    cross[128:256, 128:256] = jnp.where(row == column, table[512:513, :], last)
    identity = jnp.where(
        lax.broadcasted_iota(jnp.int32, (HALF, LANES), 0)
        == lax.broadcasted_iota(jnp.int32, (HALF, LANES), 1) % HALF,
        1.0,
        0.0,
    )
    halves = (slice(0, HALF), slice(HALF, PROBES))
    for wave in range(ITERS + 2):
        work = [(half, wave - half) for half in (0, 1) if 0 <= wave - half <= ITERS]
        gram, rows = 0.0, []
        for half, stage in work:
            sides = (half,) if len(work) == 2 else (0, 1)
            x = sketch[stage, halves[half], :]
            for side in sides:
                gram = gram + exact_dot(x, padded(x, side), 1, 1)
            if half == 1:
                before = basis[stage, halves[0], :]
                overlap = exact_dot(x, before, 1, 1)
                for side in sides:
                    gram = gram - exact_dot(overlap, padded(overlap, side), 1, 1)
                x = x - exact_dot(overlap, before, 1, 0)
            rows.append(x)
        moved = exact_dot(jnp.concatenate(rows, axis=0), cross[...], 1, 0)
        gram_rows = [gram[SUB * g : SUB * g + SUB, :] for g in range(HALF // SUB)]
        inverse_rows = [identity[SUB * g : SUB * g + SUB, :] for g in range(HALF // SUB)]
        own = own_columns(gram_rows, 0)
        for g in range(HALF // SUB):
            own = eliminate_panel(gram_rows, inverse_rows, g, own)
        inverse = jnp.concatenate(inverse_rows, axis=0)
        for at, (half, stage) in enumerate(work):
            both = jnp.concatenate([rows[at], moved[HALF * at : HALF * at + HALF, :]], axis=1)
            done = exact_dot(inverse[:, halves[half]], both, 1, 0)
            basis[stage, halves[half], :] = done[:, :PANEL]
            if stage < ITERS:
                sketch[stage + 1, halves[half], :] = done[:, PANEL:]
    final = basis[ITERS].astype(jnp.bfloat16)
    for layer, sens in enumerate((sens_low, sens_high)):
        for s in range(SUB):
            at = 1024 * layer + 128 * s
            parts[:, at : at + 128] = dot(final, sens[s], 1, 0).astype(jnp.bfloat16)


def brick_moves(step):
    devices = lax.axis_size("brick")
    return [(i, step(i)) for i in range(devices)]


def coordinates(index):
    return index // 8, index // 2 % 4, index % 2


def across_cores():
    return brick_moves(lambda i: i ^ 1)


def pick(parts, index):
    return lax.dynamic_index_in_dim(parts, index, 0, keepdims=False)


def pairs(i, step):
    return i ^ 1 if step == 0 else 3 - i


def pair_x(step):
    return brick_moves(lambda i: pairs(i // 8, step) * 8 + i % 8)


def pair_z(step):
    return brick_moves(lambda i: i // 8 * 8 + pairs(i % 8 // 2, step) * 2 + i % 2)


def halved(table, keep, move):
    parts = table.reshape(2, -1, 128)
    return pick(parts, keep) + lax.ppermute(pick(parts, 1 - keep), "brick", move)


def doubled(part, kept, move):
    other = lax.ppermute(part, "brick", move)
    return jnp.where(kept == 0, jnp.concatenate([part, other]), jnp.concatenate([other, part]))


def brick_sum(table):
    x, _, core = coordinates(lax.axis_index("brick"))
    inner = ((x == 1) | (x == 2)).astype(jnp.int32)
    moves = [pair_x(0), across_cores(), brick_moves(lambda i: pairs(i // 8, 0) * 8 + (i % 8 ^ 1))]
    quarters = table.reshape(4, -1, 128)
    place = core * 2 + inner
    part = pick(quarters, place)
    got = [lax.ppermute(pick(quarters, place ^ (k + 1)), "brick", moves[k]) for k in range(3)]
    part = (part + got[0]) + (got[1] + got[2])
    part = part + lax.ppermute(part, "brick", pair_x(1))
    part = part + lax.ppermute(part, "brick", pair_z(0))
    part = part + lax.ppermute(part, "brick", pair_z(1))
    got = [lax.ppermute(part, "brick", move) for move in moves]
    own = jnp.where(inner == 0, jnp.concatenate([part, got[0]]), jnp.concatenate([got[0], part]))
    other = jnp.where(inner == 0, jnp.concatenate(got[1:]), jnp.concatenate(got[:0:-1]))
    return jnp.where(core == 0, jnp.concatenate([own, other]), jnp.concatenate([other, own]))


def shape(*dims, dtype=jnp.float32):
    return jax.ShapeDtypeStruct(dims, dtype)


def local(forward, adjoint, probes, datum):
    fwd, adj = tiled(forward), tiled(adjoint)
    layer = (SUB, PANEL, LANES)
    anywhere = pl.BlockSpec(memory_space=pl.ANY)
    lowest = pl.pallas_call(
        upper_kernel,
        in_specs=[WHOLE, anywhere, anywhere],
        out_specs=WHOLE,
        out_shape=shape(*layer, dtype=jnp.bfloat16),
        scratch_shapes=[pltpu.VMEM((PANEL * SUB, LANES), jnp.float32)] + row_scratch(4),
        compiler_params=pltpu.CompilerParams(vmem_limit_bytes=60 * 1024 * 1024),
        cost_estimate=cost(10_000_000, 8_000_000),
        name="upper",
    )(datum, fwd, adj)
    devices = range(lax.axis_size("brick"))
    above = lax.ppermute(lowest, "brick", [(i + 1, i) for i in devices if i + 1 in devices])
    sens_low, rest = pl.pallas_call(
        side_kernel,
        in_specs=[WHOLE, anywhere, anywhere],
        out_specs=(WHOLE, WHOLE),
        out_shape=(shape(*layer, dtype=jnp.bfloat16), shape(*layer)),
        scratch_shapes=[pltpu.VMEM((PANEL * SUB, LANES), jnp.float32)] * 2 + row_scratch(6),
        compiler_params=PARAMS,
        cost_estimate=cost(20_000_000, 30_000_000),
        name="side",
    )(datum, fwd, adj)
    low_cross, low_sketch = pl.pallas_call(
        low_sums_kernel,
        in_specs=[WHOLE] * 2,
        out_specs=(WHOLE, WHOLE),
        out_shape=(shape(PANEL, PANEL), shape(PROBES, PANEL)),
        compiler_params=PARAMS,
        cost_estimate=cost(200_000_000, 3_000_000),
        name="low_sums",
    )(sens_low, probes)
    sens_high, table = pl.pallas_call(
        high_sums_kernel,
        in_specs=[WHOLE] * 5,
        out_specs=(WHOLE, WHOLE),
        out_shape=(shape(*layer, dtype=jnp.bfloat16), shape(544, 128)),
        compiler_params=PARAMS,
        cost_estimate=cost(200_000_000, 3_000_000),
        name="high_sums",
    )(rest, above, probes, low_cross, low_sketch)
    table = brick_sum(table)
    parts = pl.pallas_call(
        basis_kernel,
        in_specs=[WHOLE] * 3,
        out_specs=WHOLE,
        out_shape=shape(PROBES, 2048, dtype=jnp.bfloat16),
        scratch_shapes=[
            pltpu.VMEM((ITERS + 1, PROBES, PANEL), jnp.float32),
            pltpu.VMEM((ITERS + 1, PROBES, PANEL), jnp.float32),
            pltpu.VMEM((PANEL, PANEL), jnp.float32),
        ],
        compiler_params=PARAMS,
        cost_estimate=cost(400_000_000, 60_000_000),
        name="basis",
    )(table, sens_low, sens_high)
    parts = lax.all_to_all(parts.reshape(8, 16, 2048), "freq", 0, 0)
    return parts.astype(jnp.float32).sum(0).reshape(16, 2, 1024)


def solution(mesh):
    return jax.shard_map(
        local,
        mesh=mesh,
        in_specs=(
            P("freq", None, None, "brick", None),
            P("freq", None, None, "brick", None),
            P("brick", None, None),
            P("freq", None),
        ),
        out_specs=P("freq", "brick", None),
        check_vma=False,
    )
```

```python
import jax
import jax.numpy as jnp
from jax import lax
from jax.experimental import pallas as pl
from jax.experimental.pallas import tpu as pltpu
from jax.sharding import PartitionSpec as P

SITES = 40
NX = 64
ITERS = 4
PANEL = 256
PROBES = 128
SUB, LANES = 8, 128
HALF = 64

WHOLE = pl.BlockSpec(memory_space=pltpu.VMEM)
SCALARS = pl.BlockSpec(memory_space=pltpu.SMEM)
PARAMS = pltpu.CompilerParams(vmem_limit_bytes=40 * 1024 * 1024)


def cost(flops, size):
    return pl.CostEstimate(flops=flops, bytes_accessed=size, transcendentals=0)


def tiled(rows):
    lead = rows.shape[1:3]
    split = rows.reshape(lead + (2, SUB, LANES))
    return jnp.transpose(split, (0, 1, 3, 2, 4)).reshape(lead + (2 * SUB, LANES))


def decode(code):
    second = (code >= 4 * SITES).astype(jnp.int32)
    rest = code - second * (4 * SITES)
    fwd_row = second * 2 + (rest & 3) // 2
    adj_row = second * (2 * SITES) + rest // 4 * 2 + (rest & 1)
    return fwd_row, adj_row


def position(axis):
    return lax.broadcasted_iota(jnp.int32, (SUB, LANES), axis)


def next_column(field):
    return jnp.where(position(1) % NX == NX - 1, 0.0, pltpu.roll(field, LANES - 1, 1))


def next_row(field):
    swapped = pltpu.roll(field, NX, 1)
    later = jnp.where(position(0) == SUB - 1, 0.0, pltpu.roll(swapped, SUB - 1, 0))
    return jnp.where(position(1) < NX, swapped, later)


def tile_rows(index, size):
    return pl.ds(pl.multiple_of(index * size, size), size)


def widen(narrow, wide, start, count, parts):
    def one(i, carry):
        for k in range(parts):
            wide[tile_rows(i * parts + k, 16), :] = narrow[i, k].astype(jnp.float32)
        return carry

    lax.fori_loop(start, start + count, one, 0, unroll=4)


def load_rows(parts, codes, fwd, adj, scratch):
    rows, row_table, fwd_narrow, adj_narrow, fwd_wide, adj_wide, done = scratch
    half = adj.shape[0] // 2
    low, high = slice(0, half), slice(half, 2 * half)
    copies = [
        pltpu.make_async_copy(adj.at[low, 0:parts], adj_narrow.at[low], done.at[0]),
        pltpu.make_async_copy(fwd.at[:, 0:parts], fwd_narrow, done.at[1]),
        pltpu.make_async_copy(adj.at[high, 0:parts], adj_narrow.at[high], done.at[2]),
    ]
    for copy in copies:
        copy.start()
    row_table[0:1, :], row_table[1:2, :] = decode(codes[...])
    table_copy = pltpu.make_async_copy(row_table, rows, done.at[3])
    table_copy.start()
    copies[1].wait()
    widen(fwd_narrow, fwd_wide, 0, fwd.shape[0], parts)
    copies[0].wait()
    widen(adj_narrow, adj_wide, 0, half, parts)
    copies[2].wait()
    widen(adj_narrow, adj_wide, half, half, parts)
    table_copy.wait()

    def product(d, orientation, layer):
        def field(wide, row, part):
            return wide[pl.ds(row * (parts * 16) + part * 16 + layer, SUB, stride=2), :]

        fwd_row, adj_row = rows[0, d], rows[1, d]
        real, imag = 2 * orientation, 2 * orientation + 1
        return field(fwd_wide, fwd_row, real) * field(adj_wide, adj_row, real) - field(
            fwd_wide, fwd_row, imag
        ) * field(adj_wide, adj_row, imag)

    return product


def row_scratch(parts):
    return [
        pltpu.SMEM((SUB, PANEL), jnp.int32),
        pltpu.VMEM((SUB, PANEL), jnp.int32),
        pltpu.VMEM((4, parts, 16, LANES), jnp.bfloat16),
        pltpu.VMEM((160, parts, 16, LANES), jnp.bfloat16),
        pltpu.VMEM((4 * parts * 16, LANES), jnp.float32),
        pltpu.VMEM((160 * parts * 16, LANES), jnp.float32),
        pltpu.SemaphoreType.DMA((4,)),
    ]


def chunk(table, block, s):
    return [table[pl.ds(block * 128 + half * 64 + s, SUB, stride=SUB), :] for half in range(2)]


def upper_kernel(codes, fwd, adj, lowest, low_upper, *scratch):
    product = load_rows(4, codes, fwd, adj, scratch)

    def one(d, carry):
        edge_x, edge_y = product(d, 0, 0), product(d, 1, 0)
        low_upper[tile_rows(d, SUB), :] = edge_x + next_row(edge_x) + (edge_y + next_column(edge_y))
        return carry

    lax.fori_loop(0, PANEL, one, 0, unroll=128)

    def block(i, carry):
        for s in range(SUB):
            piece = jnp.concatenate(chunk(low_upper, i, s), axis=0)
            lowest[s, tile_rows(i, 16), :] = piece.astype(jnp.bfloat16)
        return carry

    lax.fori_loop(0, PANEL // 16, block, 0, unroll=2)


def side_kernel(codes, fwd, adj, sens, rest, low, high, *scratch):
    product = load_rows(6, codes, fwd, adj, scratch)

    def one(d, carry):
        edge_x, edge_y, edge_z = [
            [product(d, orientation, layer) for layer in range(2)] for orientation in range(3)
        ]
        paired = [edge + next_column(edge) for edge in edge_z]
        across = edge_y[1] + next_column(edge_y[1])
        both = edge_y[0] + next_column(edge_y[0]) + across
        down = [edge_x[0] + edge_x[1] + paired[0], edge_x[1] + paired[1]]
        low[tile_rows(d, SUB), :] = both + (down[0] + next_row(down[0]))
        high[tile_rows(d, SUB), :] = across + (down[1] + next_row(down[1]))
        return carry

    lax.fori_loop(0, PANEL, one, 0, unroll=16)

    def block(i, carry):
        for s in range(SUB):
            piece = jnp.concatenate(chunk(low, i, s), axis=0)
            sens[s, tile_rows(i, 16), :] = (0.25 * piece).astype(jnp.bfloat16)
            pieces = chunk(high, i, s)
            rest[s, tile_rows(2 * i, SUB), :] = pieces[0]
            rest[s, tile_rows(2 * i + 1, SUB), :] = pieces[1]
        return carry

    lax.fori_loop(0, PANEL // 16, block, 0, unroll=2)


def dot(left, right, left_dim, right_dim, precision=None):
    return lax.dot_general(
        left,
        right,
        (((left_dim,), (right_dim,)), ((), ())),
        precision=precision,
        preferred_element_type=jnp.float32,
    )


def layer_sums(sens, probes, layer):
    cross, sketch = 0.0, 0.0
    for s in range(0, SUB, 2):
        pair = jnp.concatenate([sens[s], sens[s + 1]], axis=1)
        cross = cross + dot(pair, pair, 1, 1)
        sketch = sketch + dot(probes[layer, 128 * s : 128 * s + 256, :], pair, 0, 1)
    return cross, sketch


def block_index(axis):
    return lax.broadcasted_iota(jnp.int32, (LANES, LANES), axis)


def low_sums_kernel(sens, probes, cross, sketch):
    cross[...], sketch[...] = layer_sums(sens, probes, 0)


def high_sums_kernel(rest, above, probes, low_cross, low_sketch, sens, table):
    def block(i, carry):
        for s in range(SUB):
            here = (s, tile_rows(i, 16), slice(None))
            sens[here] = (0.25 * (rest[here] + above[here].astype(jnp.float32))).astype(jnp.bfloat16)
        return carry

    lax.fori_loop(0, PANEL // 16, block, 0)
    cross, sketch = layer_sums(sens, probes, 1)
    cross, sketch = cross + low_cross[...], sketch + low_sketch[...]
    table[0:128, :], table[128:256, :] = sketch[:, :128], sketch[:, 128:]
    table[256:384, :] = cross[:128, 128:]
    last = cross[128:, 128:]
    table[384:512, :] = jnp.where(block_index(0) <= block_index(1), cross[:128, :128], last)
    diagonal = jnp.sum(jnp.where(block_index(0) == block_index(1), last, 0.0), axis=0, keepdims=True)
    table[512:544, :] = jnp.broadcast_to(diagonal, (32, LANES))


def spread(piece):
    return jnp.broadcast_to(piece, (SUB, LANES))


def column_of_each(piece, at):
    left = lax.broadcasted_iota(jnp.int32, (SUB, LANES), 1) < HALF
    return jnp.where(left, spread(piece[:, at : at + 1]), spread(piece[:, HALF + at : HALF + at + 1]))


def own_columns(gram, g):
    return [column_of_each(gram[g], SUB * g + k) for k in range(SUB)]


def eliminate_panel(gram, inverse, g, own):
    row = lax.broadcasted_iota(jnp.int32, (SUB, LANES), 0)
    later = range(g + 1, len(gram))
    column = {(q, k): column_of_each(gram[q], SUB * g + k) for q in later for k in range(SUB)}
    following = own_columns(gram, g + 1) if later else None
    u = {(i, k): spread(own[k][i : i + 1, :]) for k in range(SUB) for i in range(k + 1)}
    root = []
    for k in range(SUB):
        root.append(lax.rsqrt(u[k, k]))
        for j in range(k + 1, SUB):
            u[k, j] = u[k, j] * root[k]
        for j in range(k + 1, SUB):
            for i in range(k + 1, j + 1):
                u[i, j] = u[i, j] - u[k, i] * u[k, j]
    low = {}
    for q in later:
        for k in range(SUB):
            entry = column[q, k]
            for j in range(k):
                entry = entry - low[q, j] * u[j, k]
            low[q, k] = entry * root[k]
    if later:
        for c in range(SUB):
            for k in range(SUB):
                across = low[g + 1, k]
                following[c] = following[c] - across * spread(across[c : c + 1, :])
    for table in (gram, inverse):
        lead = [spread(table[g][k : k + 1, :]) for k in range(SUB)]
        for k in range(SUB):
            for j in range(k):
                lead[k] = lead[k] - u[j, k] * lead[j]
            lead[k] = lead[k] * root[k]
        table[g] = lead[0]
        for k in range(1, SUB):
            table[g] = jnp.where(row == k, lead[k], table[g])
        for q in later:
            for k in range(SUB):
                table[q] = table[q] - low[q, k] * lead[k]
    return following


def exact_dot(left, right, left_dim, right_dim):
    return dot(left, right, left_dim, right_dim, lax.Precision.HIGHEST)


def padded(block, side):
    zeros = jnp.zeros_like(block)
    return jnp.concatenate([zeros, block] if side else [block, zeros], axis=0)


def basis_kernel(table, sens_low, sens_high, parts, basis, sketch, cross):
    sketch[0, :, 0:128], sketch[0, :, 128:256] = table[0:128, :], table[128:256, :]
    corner, packed = table[256:384, :], table[384:512, :]
    turned = packed.T
    row, column = block_index(0), block_index(1)
    cross[0:128, 0:128] = jnp.where(row <= column, packed, turned)
    cross[0:128, 128:256] = corner
    cross[128:256, 0:128] = corner.T
    last = jnp.where(row > column, packed, turned)
    cross[128:256, 128:256] = jnp.where(row == column, table[512:513, :], last)
    identity = jnp.where(
        lax.broadcasted_iota(jnp.int32, (HALF, LANES), 0)
        == lax.broadcasted_iota(jnp.int32, (HALF, LANES), 1) % HALF,
        1.0,
        0.0,
    )
    halves = (slice(0, HALF), slice(HALF, PROBES))
    for wave in range(ITERS + 2):
        work = [(half, wave - half) for half in (0, 1) if 0 <= wave - half <= ITERS]
        gram, rows = 0.0, []
        for half, stage in work:
            sides = (half,) if len(work) == 2 else (0, 1)
            x = sketch[stage, halves[half], :]
            for side in sides:
                gram = gram + exact_dot(x, padded(x, side), 1, 1)
            if half == 1:
                before = basis[stage, halves[0], :]
                overlap = exact_dot(x, before, 1, 1)
                for side in sides:
                    gram = gram - exact_dot(overlap, padded(overlap, side), 1, 1)
                x = x - exact_dot(overlap, before, 1, 0)
            rows.append(x)
        moved = exact_dot(jnp.concatenate(rows, axis=0), cross[...], 1, 0)
        gram_rows = [gram[SUB * g : SUB * g + SUB, :] for g in range(HALF // SUB)]
        inverse_rows = [identity[SUB * g : SUB * g + SUB, :] for g in range(HALF // SUB)]
        own = own_columns(gram_rows, 0)
        for g in range(HALF // SUB):
            own = eliminate_panel(gram_rows, inverse_rows, g, own)
        inverse = jnp.concatenate(inverse_rows, axis=0)
        for at, (half, stage) in enumerate(work):
            both = jnp.concatenate([rows[at], moved[HALF * at : HALF * at + HALF, :]], axis=1)
            done = exact_dot(inverse[:, halves[half]], both, 1, 0)
            basis[stage, halves[half], :] = done[:, :PANEL]
            if stage < ITERS:
                sketch[stage + 1, halves[half], :] = done[:, PANEL:]
    final = basis[ITERS].astype(jnp.bfloat16)
    for layer, sens in enumerate((sens_low, sens_high)):
        for s in range(0, SUB, 2):
            at = 1024 * layer + 128 * s
            pair = jnp.concatenate([sens[s], sens[s + 1]], axis=1)
            parts[:, at : at + 256] = dot(final, pair, 1, 0).astype(jnp.bfloat16)


def brick_moves(step):
    devices = lax.axis_size("brick")
    return [(i, step(i)) for i in range(devices)]


def coordinates(index):
    return index // 8, index // 2 % 4, index % 2


def across_cores():
    return brick_moves(lambda i: i ^ 1)


def pick(parts, index):
    return lax.dynamic_index_in_dim(parts, index, 0, keepdims=False)


def pairs(i, step):
    return i ^ 1 if step == 0 else 3 - i


def pair_x(step):
    return brick_moves(lambda i: pairs(i // 8, step) * 8 + i % 8)


def pair_z(step):
    return brick_moves(lambda i: i // 8 * 8 + pairs(i % 8 // 2, step) * 2 + i % 2)


def halved(table, keep, move):
    parts = table.reshape(2, -1, 128)
    return pick(parts, keep) + lax.ppermute(pick(parts, 1 - keep), "brick", move)


def doubled(part, kept, move):
    other = lax.ppermute(part, "brick", move)
    return jnp.where(kept == 0, jnp.concatenate([part, other]), jnp.concatenate([other, part]))


def brick_sum(table):
    x, _, core = coordinates(lax.axis_index("brick"))
    inner = ((x == 1) | (x == 2)).astype(jnp.int32)
    moves = [pair_x(0), across_cores(), brick_moves(lambda i: pairs(i // 8, 0) * 8 + (i % 8 ^ 1))]
    quarters = table.reshape(4, -1, 128)
    place = core * 2 + inner
    part = pick(quarters, place)
    got = [lax.ppermute(pick(quarters, place ^ (k + 1)), "brick", moves[k]) for k in range(3)]
    part = (part + got[0]) + (got[1] + got[2])
    part = part + lax.ppermute(part, "brick", pair_x(1))
    part = part + lax.ppermute(part, "brick", pair_z(0))
    part = part + lax.ppermute(part, "brick", pair_z(1))
    got = [lax.ppermute(part, "brick", move) for move in moves]
    own = jnp.where(inner == 0, jnp.concatenate([part, got[0]]), jnp.concatenate([got[0], part]))
    other = jnp.where(inner == 0, jnp.concatenate(got[1:]), jnp.concatenate(got[:0:-1]))
    return jnp.where(core == 0, jnp.concatenate([own, other]), jnp.concatenate([other, own]))


def shape(*dims, dtype=jnp.float32):
    return jax.ShapeDtypeStruct(dims, dtype)


def local(forward, adjoint, probes, datum):
    fwd, adj = tiled(forward), tiled(adjoint)
    layer = (SUB, PANEL, LANES)
    anywhere = pl.BlockSpec(memory_space=pl.ANY)
    lowest = pl.pallas_call(
        upper_kernel,
        in_specs=[WHOLE, anywhere, anywhere],
        out_specs=WHOLE,
        out_shape=shape(*layer, dtype=jnp.bfloat16),
        scratch_shapes=[pltpu.VMEM((PANEL * SUB, LANES), jnp.float32)] + row_scratch(4),
        compiler_params=pltpu.CompilerParams(vmem_limit_bytes=60 * 1024 * 1024),
        cost_estimate=cost(10_000_000, 8_000_000),
        name="upper",
    )(datum, fwd, adj)
    devices = range(lax.axis_size("brick"))
    above = lax.ppermute(lowest, "brick", [(i + 1, i) for i in devices if i + 1 in devices])
    sens_low, rest = pl.pallas_call(
        side_kernel,
        in_specs=[WHOLE, anywhere, anywhere],
        out_specs=(WHOLE, WHOLE),
        out_shape=(shape(*layer, dtype=jnp.bfloat16), shape(*layer)),
        scratch_shapes=[pltpu.VMEM((PANEL * SUB, LANES), jnp.float32)] * 2 + row_scratch(6),
        compiler_params=PARAMS,
        cost_estimate=cost(20_000_000, 30_000_000),
        name="side",
    )(datum, fwd, adj)
    low_cross, low_sketch = pl.pallas_call(
        low_sums_kernel,
        in_specs=[WHOLE] * 2,
        out_specs=(WHOLE, WHOLE),
        out_shape=(shape(PANEL, PANEL), shape(PROBES, PANEL)),
        compiler_params=PARAMS,
        cost_estimate=cost(200_000_000, 3_000_000),
        name="low_sums",
    )(sens_low, probes)
    sens_high, table = pl.pallas_call(
        high_sums_kernel,
        in_specs=[WHOLE] * 5,
        out_specs=(WHOLE, WHOLE),
        out_shape=(shape(*layer, dtype=jnp.bfloat16), shape(544, 128)),
        compiler_params=PARAMS,
        cost_estimate=cost(200_000_000, 3_000_000),
        name="high_sums",
    )(rest, above, probes, low_cross, low_sketch)
    table = brick_sum(table)
    parts = pl.pallas_call(
        basis_kernel,
        in_specs=[WHOLE] * 3,
        out_specs=WHOLE,
        out_shape=shape(PROBES, 2048, dtype=jnp.bfloat16),
        scratch_shapes=[
            pltpu.VMEM((ITERS + 1, PROBES, PANEL), jnp.float32),
            pltpu.VMEM((ITERS + 1, PROBES, PANEL), jnp.float32),
            pltpu.VMEM((PANEL, PANEL), jnp.float32),
        ],
        compiler_params=PARAMS,
        cost_estimate=cost(400_000_000, 60_000_000),
        name="basis",
    )(table, sens_low, sens_high)
    parts = lax.all_to_all(parts.reshape(8, 16, 2048), "freq", 0, 0)
    return parts.astype(jnp.float32).sum(0).reshape(16, 2, 1024)


def solution(mesh):
    return jax.shard_map(
        local,
        mesh=mesh,
        in_specs=(
            P("freq", None, None, "brick", None),
            P("freq", None, None, "brick", None),
            P("brick", None, None),
            P("freq", None),
        ),
        out_specs=P("freq", "brick", None),
        check_vma=False,
    )
```

```python
import jax
import jax.numpy as jnp
from jax import lax
from jax.experimental import pallas as pl
from jax.experimental.pallas import tpu as pltpu
from jax.sharding import PartitionSpec as P

SITES = 40
NX = 64
ITERS = 4
PANEL = 256
PROBES = 128
SUB, LANES = 8, 128
HALF = 64

WHOLE = pl.BlockSpec(memory_space=pltpu.VMEM)
SCALARS = pl.BlockSpec(memory_space=pltpu.SMEM)
PARAMS = pltpu.CompilerParams(vmem_limit_bytes=40 * 1024 * 1024)


def cost(flops, size):
    return pl.CostEstimate(flops=flops, bytes_accessed=size, transcendentals=0)


def tiled(rows):
    lead = rows.shape[1:3]
    split = rows.reshape(lead + (2, SUB, LANES))
    return jnp.transpose(split, (0, 1, 3, 2, 4)).reshape(lead + (2 * SUB, LANES))


def decode(code):
    second = (code >= 4 * SITES).astype(jnp.int32)
    rest = code - second * (4 * SITES)
    fwd_row = second * 2 + (rest & 3) // 2
    adj_row = second * (2 * SITES) + rest // 4 * 2 + (rest & 1)
    return fwd_row, adj_row


def position(axis):
    return lax.broadcasted_iota(jnp.int32, (SUB, LANES), axis)


def next_column(field):
    return jnp.where(position(1) % NX == NX - 1, 0.0, pltpu.roll(field, LANES - 1, 1))


def next_row(field):
    swapped = pltpu.roll(field, NX, 1)
    later = jnp.where(position(0) == SUB - 1, 0.0, pltpu.roll(swapped, SUB - 1, 0))
    return jnp.where(position(1) < NX, swapped, later)


def tile_rows(index, size):
    return pl.ds(pl.multiple_of(index * size, size), size)


def widen(narrow, wide, start, count, parts):
    def one(i, carry):
        for k in range(parts):
            wide[tile_rows(i * parts + k, 16), :] = narrow[i, k].astype(jnp.float32)
        return carry

    lax.fori_loop(start, start + count, one, 0, unroll=4)


def load_rows(parts, codes, fwd, adj, scratch):
    rows, row_table, fwd_narrow, adj_narrow, fwd_wide, adj_wide, done = scratch
    half = adj.shape[0] // 2
    low, high = slice(0, half), slice(half, 2 * half)
    copies = [
        pltpu.make_async_copy(adj.at[low, 0:parts], adj_narrow.at[low], done.at[0]),
        pltpu.make_async_copy(fwd.at[:, 0:parts], fwd_narrow, done.at[1]),
        pltpu.make_async_copy(adj.at[high, 0:parts], adj_narrow.at[high], done.at[2]),
    ]
    for copy in copies:
        copy.start()
    row_table[0:1, :], row_table[1:2, :] = decode(codes[...])
    table_copy = pltpu.make_async_copy(row_table, rows, done.at[3])
    table_copy.start()
    copies[1].wait()
    widen(fwd_narrow, fwd_wide, 0, fwd.shape[0], parts)
    copies[0].wait()
    widen(adj_narrow, adj_wide, 0, half, parts)
    copies[2].wait()
    widen(adj_narrow, adj_wide, half, half, parts)
    table_copy.wait()

    def product(d, orientation, layer):
        def field(wide, row, part):
            return wide[pl.ds(row * (parts * 16) + part * 16 + layer, SUB, stride=2), :]

        fwd_row, adj_row = rows[0, d], rows[1, d]
        real, imag = 2 * orientation, 2 * orientation + 1
        return field(fwd_wide, fwd_row, real) * field(adj_wide, adj_row, real) - field(
            fwd_wide, fwd_row, imag
        ) * field(adj_wide, adj_row, imag)

    return product


def row_scratch(parts):
    return [
        pltpu.SMEM((SUB, PANEL), jnp.int32),
        pltpu.VMEM((SUB, PANEL), jnp.int32),
        pltpu.VMEM((4, parts, 16, LANES), jnp.bfloat16),
        pltpu.VMEM((160, parts, 16, LANES), jnp.bfloat16),
        pltpu.VMEM((4 * parts * 16, LANES), jnp.float32),
        pltpu.VMEM((160 * parts * 16, LANES), jnp.float32),
        pltpu.SemaphoreType.DMA((4,)),
    ]


def chunk(table, block, s):
    return [table[pl.ds(block * 128 + half * 64 + s, SUB, stride=SUB), :] for half in range(2)]


def upper_kernel(codes, fwd, adj, lowest, low_upper, *scratch):
    product = load_rows(4, codes, fwd, adj, scratch)

    def one(d, carry):
        edge_x, edge_y = product(d, 0, 0), product(d, 1, 0)
        low_upper[tile_rows(d, SUB), :] = edge_x + next_row(edge_x) + (edge_y + next_column(edge_y))
        return carry

    lax.fori_loop(0, PANEL, one, 0, unroll=128)

    def block(i, carry):
        for s in range(SUB):
            piece = jnp.concatenate(chunk(low_upper, i, s), axis=0)
            lowest[s, tile_rows(i, 16), :] = piece.astype(jnp.bfloat16)
        return carry

    lax.fori_loop(0, PANEL // 16, block, 0, unroll=2)


def side_kernel(codes, fwd, adj, sens, rest, low, high, *scratch):
    product = load_rows(6, codes, fwd, adj, scratch)

    def one(d, carry):
        edge_x, edge_y, edge_z = [
            [product(d, orientation, layer) for layer in range(2)] for orientation in range(3)
        ]
        paired = [edge + next_column(edge) for edge in edge_z]
        across = edge_y[1] + next_column(edge_y[1])
        both = edge_y[0] + next_column(edge_y[0]) + across
        down = [edge_x[0] + edge_x[1] + paired[0], edge_x[1] + paired[1]]
        low[tile_rows(d, SUB), :] = both + (down[0] + next_row(down[0]))
        high[tile_rows(d, SUB), :] = across + (down[1] + next_row(down[1]))
        return carry

    lax.fori_loop(0, PANEL, one, 0, unroll=16)

    def block(i, carry):
        for s in range(SUB):
            piece = jnp.concatenate(chunk(low, i, s), axis=0)
            sens[s, tile_rows(i, 16), :] = (0.25 * piece).astype(jnp.bfloat16)
            pieces = chunk(high, i, s)
            rest[s, tile_rows(2 * i, SUB), :] = pieces[0]
            rest[s, tile_rows(2 * i + 1, SUB), :] = pieces[1]
        return carry

    lax.fori_loop(0, PANEL // 16, block, 0, unroll=2)


def dot(left, right, left_dim, right_dim, precision=None):
    return lax.dot_general(
        left,
        right,
        (((left_dim,), (right_dim,)), ((), ())),
        precision=precision,
        preferred_element_type=jnp.float32,
    )


def layer_sums(sens, probes, layer):
    cross, sketch = 0.0, 0.0
    for s in range(0, SUB, 2):
        pair = jnp.concatenate([sens[s], sens[s + 1]], axis=1)
        cross = cross + dot(pair, pair, 1, 1)
        sketch = sketch + dot(probes[layer, 128 * s : 128 * s + 256, :], pair, 0, 1)
    return cross, sketch


def block_index(axis):
    return lax.broadcasted_iota(jnp.int32, (LANES, LANES), axis)


def low_sums_kernel(sens, probes, cross, sketch):
    cross[...], sketch[...] = layer_sums(sens, probes, 0)


def high_sums_kernel(rest, above, probes, low_cross, low_sketch, sens, table):
    def block(i, carry):
        for s in range(SUB):
            here = (s, tile_rows(i, 16), slice(None))
            sens[here] = (0.25 * (rest[here] + above[here].astype(jnp.float32))).astype(jnp.bfloat16)
        return carry

    lax.fori_loop(0, PANEL // 16, block, 0, unroll=4)
    cross, sketch = layer_sums(sens, probes, 1)
    cross, sketch = cross + low_cross[...], sketch + low_sketch[...]
    table[0:128, :], table[128:256, :] = sketch[:, :128], sketch[:, 128:]
    table[256:384, :] = cross[:128, 128:]
    last = cross[128:, 128:]
    table[384:512, :] = jnp.where(block_index(0) <= block_index(1), cross[:128, :128], last)
    diagonal = jnp.sum(jnp.where(block_index(0) == block_index(1), last, 0.0), axis=0, keepdims=True)
    table[512:544, :] = jnp.broadcast_to(diagonal, (32, LANES))


def spread(piece):
    return jnp.broadcast_to(piece, (SUB, LANES))


def column_of_each(piece, at):
    left = lax.broadcasted_iota(jnp.int32, (SUB, LANES), 1) < HALF
    return jnp.where(left, spread(piece[:, at : at + 1]), spread(piece[:, HALF + at : HALF + at + 1]))


def own_columns(gram, g):
    return [column_of_each(gram[g], SUB * g + k) for k in range(SUB)]


def eliminate_panel(gram, inverse, g, own):
    row = lax.broadcasted_iota(jnp.int32, (SUB, LANES), 0)
    later = range(g + 1, len(gram))
    column = {(q, k): column_of_each(gram[q], SUB * g + k) for q in later for k in range(SUB)}
    following = own_columns(gram, g + 1) if later else None
    u = {(i, k): spread(own[k][i : i + 1, :]) for k in range(SUB) for i in range(k + 1)}
    root = []
    for k in range(SUB):
        root.append(lax.rsqrt(u[k, k]))
        for j in range(k + 1, SUB):
            u[k, j] = u[k, j] * root[k]
        for j in range(k + 1, SUB):
            for i in range(k + 1, j + 1):
                u[i, j] = u[i, j] - u[k, i] * u[k, j]
    low = {}
    for q in later:
        for k in range(SUB):
            entry = column[q, k]
            for j in range(k):
                entry = entry - low[q, j] * u[j, k]
            low[q, k] = entry * root[k]
    if later:
        for c in range(SUB):
            for k in range(SUB):
                across = low[g + 1, k]
                following[c] = following[c] - across * spread(across[c : c + 1, :])
    for table in (gram, inverse):
        lead = [spread(table[g][k : k + 1, :]) for k in range(SUB)]
        for k in range(SUB):
            for j in range(k):
                lead[k] = lead[k] - u[j, k] * lead[j]
            lead[k] = lead[k] * root[k]
        table[g] = lead[0]
        for k in range(1, SUB):
            table[g] = jnp.where(row == k, lead[k], table[g])
        for q in later:
            for k in range(SUB):
                table[q] = table[q] - low[q, k] * lead[k]
    return following


def exact_dot(left, right, left_dim, right_dim):
    return dot(left, right, left_dim, right_dim, lax.Precision.HIGHEST)


def padded(block, side):
    zeros = jnp.zeros_like(block)
    return jnp.concatenate([zeros, block] if side else [block, zeros], axis=0)


def basis_kernel(table, sens_low, sens_high, parts, basis, sketch, cross):
    sketch[0, :, 0:128], sketch[0, :, 128:256] = table[0:128, :], table[128:256, :]
    corner, packed = table[256:384, :], table[384:512, :]
    turned = packed.T
    row, column = block_index(0), block_index(1)
    cross[0:128, 0:128] = jnp.where(row <= column, packed, turned)
    cross[0:128, 128:256] = corner
    cross[128:256, 0:128] = corner.T
    last = jnp.where(row > column, packed, turned)
    cross[128:256, 128:256] = jnp.where(row == column, table[512:513, :], last)
    identity = jnp.where(
        lax.broadcasted_iota(jnp.int32, (HALF, LANES), 0)
        == lax.broadcasted_iota(jnp.int32, (HALF, LANES), 1) % HALF,
        1.0,
        0.0,
    )
    halves = (slice(0, HALF), slice(HALF, PROBES))
    for wave in range(ITERS + 2):
        work = [(half, wave - half) for half in (0, 1) if 0 <= wave - half <= ITERS]
        gram, rows = 0.0, []
        for half, stage in work:
            sides = (half,) if len(work) == 2 else (0, 1)
            x = sketch[stage, halves[half], :]
            for side in sides:
                gram = gram + exact_dot(x, padded(x, side), 1, 1)
            if half == 1:
                before = basis[stage, halves[0], :]
                overlap = exact_dot(x, before, 1, 1)
                for side in sides:
                    gram = gram - exact_dot(overlap, padded(overlap, side), 1, 1)
                x = x - exact_dot(overlap, before, 1, 0)
            rows.append(x)
        moved = exact_dot(jnp.concatenate(rows, axis=0), cross[...], 1, 0)
        gram_rows = [gram[SUB * g : SUB * g + SUB, :] for g in range(HALF // SUB)]
        inverse_rows = [identity[SUB * g : SUB * g + SUB, :] for g in range(HALF // SUB)]
        own = own_columns(gram_rows, 0)
        for g in range(HALF // SUB):
            own = eliminate_panel(gram_rows, inverse_rows, g, own)
        inverse = jnp.concatenate(inverse_rows, axis=0)
        for at, (half, stage) in enumerate(work):
            both = jnp.concatenate([rows[at], moved[HALF * at : HALF * at + HALF, :]], axis=1)
            done = exact_dot(inverse[:, halves[half]], both, 1, 0)
            basis[stage, halves[half], :] = done[:, :PANEL]
            if stage < ITERS:
                sketch[stage + 1, halves[half], :] = done[:, PANEL:]
    final = basis[ITERS].astype(jnp.bfloat16)
    for layer, sens in enumerate((sens_low, sens_high)):
        for s in range(0, SUB, 2):
            at = 1024 * layer + 128 * s
            pair = jnp.concatenate([sens[s], sens[s + 1]], axis=1)
            parts[:, at : at + 256] = dot(final, pair, 1, 0).astype(jnp.bfloat16)


def brick_moves(step):
    devices = lax.axis_size("brick")
    return [(i, step(i)) for i in range(devices)]


def coordinates(index):
    return index // 8, index // 2 % 4, index % 2


def across_cores():
    return brick_moves(lambda i: i ^ 1)


def pick(parts, index):
    return lax.dynamic_index_in_dim(parts, index, 0, keepdims=False)


def pairs(i, step):
    return i ^ 1 if step == 0 else 3 - i


def pair_x(step):
    return brick_moves(lambda i: pairs(i // 8, step) * 8 + i % 8)


def pair_z(step):
    return brick_moves(lambda i: i // 8 * 8 + pairs(i % 8 // 2, step) * 2 + i % 2)


def halved(table, keep, move):
    parts = table.reshape(2, -1, 128)
    return pick(parts, keep) + lax.ppermute(pick(parts, 1 - keep), "brick", move)


def doubled(part, kept, move):
    other = lax.ppermute(part, "brick", move)
    return jnp.where(kept == 0, jnp.concatenate([part, other]), jnp.concatenate([other, part]))


def brick_sum(table):
    x, _, core = coordinates(lax.axis_index("brick"))
    inner = ((x == 1) | (x == 2)).astype(jnp.int32)
    moves = [pair_x(0), across_cores(), brick_moves(lambda i: pairs(i // 8, 0) * 8 + (i % 8 ^ 1))]
    quarters = table.reshape(4, -1, 128)
    place = core * 2 + inner
    part = pick(quarters, place)
    got = [lax.ppermute(pick(quarters, place ^ (k + 1)), "brick", moves[k]) for k in range(3)]
    part = (part + got[0]) + (got[1] + got[2])
    part = part + lax.ppermute(part, "brick", pair_x(1))
    part = part + lax.ppermute(part, "brick", pair_z(0))
    part = part + lax.ppermute(part, "brick", pair_z(1))
    got = [lax.ppermute(part, "brick", move) for move in moves]
    own = jnp.where(inner == 0, jnp.concatenate([part, got[0]]), jnp.concatenate([got[0], part]))
    other = jnp.where(inner == 0, jnp.concatenate(got[1:]), jnp.concatenate(got[:0:-1]))
    return jnp.where(core == 0, jnp.concatenate([own, other]), jnp.concatenate([other, own]))


def shape(*dims, dtype=jnp.float32):
    return jax.ShapeDtypeStruct(dims, dtype)


def local(forward, adjoint, probes, datum):
    fwd, adj = tiled(forward), tiled(adjoint)
    layer = (SUB, PANEL, LANES)
    anywhere = pl.BlockSpec(memory_space=pl.ANY)
    lowest = pl.pallas_call(
        upper_kernel,
        in_specs=[WHOLE, anywhere, anywhere],
        out_specs=WHOLE,
        out_shape=shape(*layer, dtype=jnp.bfloat16),
        scratch_shapes=[pltpu.VMEM((PANEL * SUB, LANES), jnp.float32)] + row_scratch(4),
        compiler_params=pltpu.CompilerParams(vmem_limit_bytes=60 * 1024 * 1024),
        cost_estimate=cost(10_000_000, 8_000_000),
        name="upper",
    )(datum, fwd, adj)
    devices = range(lax.axis_size("brick"))
    above = lax.ppermute(lowest, "brick", [(i + 1, i) for i in devices if i + 1 in devices])
    sens_low, rest = pl.pallas_call(
        side_kernel,
        in_specs=[WHOLE, anywhere, anywhere],
        out_specs=(WHOLE, WHOLE),
        out_shape=(shape(*layer, dtype=jnp.bfloat16), shape(*layer)),
        scratch_shapes=[pltpu.VMEM((PANEL * SUB, LANES), jnp.float32)] * 2 + row_scratch(6),
        compiler_params=PARAMS,
        cost_estimate=cost(20_000_000, 30_000_000),
        name="side",
    )(datum, fwd, adj)
    low_cross, low_sketch = pl.pallas_call(
        low_sums_kernel,
        in_specs=[WHOLE] * 2,
        out_specs=(WHOLE, WHOLE),
        out_shape=(shape(PANEL, PANEL), shape(PROBES, PANEL)),
        compiler_params=PARAMS,
        cost_estimate=cost(200_000_000, 3_000_000),
        name="low_sums",
    )(sens_low, probes)
    sens_high, table = pl.pallas_call(
        high_sums_kernel,
        in_specs=[WHOLE] * 5,
        out_specs=(WHOLE, WHOLE),
        out_shape=(shape(*layer, dtype=jnp.bfloat16), shape(544, 128)),
        compiler_params=PARAMS,
        cost_estimate=cost(200_000_000, 3_000_000),
        name="high_sums",
    )(rest, above, probes, low_cross, low_sketch)
    table = brick_sum(table)
    parts = pl.pallas_call(
        basis_kernel,
        in_specs=[WHOLE] * 3,
        out_specs=WHOLE,
        out_shape=shape(PROBES, 2048, dtype=jnp.bfloat16),
        scratch_shapes=[
            pltpu.VMEM((ITERS + 1, PROBES, PANEL), jnp.float32),
            pltpu.VMEM((ITERS + 1, PROBES, PANEL), jnp.float32),
            pltpu.VMEM((PANEL, PANEL), jnp.float32),
        ],
        compiler_params=PARAMS,
        cost_estimate=cost(400_000_000, 60_000_000),
        name="basis",
    )(table, sens_low, sens_high)
    parts = lax.all_to_all(parts.reshape(8, 16, 2048), "freq", 0, 0)
    return parts.astype(jnp.float32).sum(0).reshape(16, 2, 1024)


def solution(mesh):
    return jax.shard_map(
        local,
        mesh=mesh,
        in_specs=(
            P("freq", None, None, "brick", None),
            P("freq", None, None, "brick", None),
            P("brick", None, None),
            P("freq", None),
        ),
        out_specs=P("freq", "brick", None),
        check_vma=False,
    )
```
